256 devices in a mesh: seq: 32 (over y, z_lo, core), dp: 8 (over x, z_hi).
Axes of the slice: x: 4, y: 4, z: 8 (z_hi: 2, z_lo: 4; z = z_hi * 4 + z_lo), core: 2. Of those that a mesh axis runs over, the one named last changes fastest.
Arguments:
- queries: bfloat16 [131072, 768], P(('dp', 'seq')), parts along dimension 0, may hold values from -400 to 400
- keys: bfloat16 [131072, 768], P(('dp', 'seq')), parts along dimension 0, may hold values from -16 to 16
- values: bfloat16 [131072, 768], P(('dp', 'seq')), parts along dimension 0, may hold values from -6 to 6
- offsets: int32 [5, 16], replicated, may hold values from 0 to 15, as said below
- out_weight: bfloat16 [768, 768], replicated, may hold values from -0.21875 to 0.21875
Outputs:
- projected: bfloat16 [131072, 768], P(('dp', 'seq')), parts along dimension 0
The draws below stay inside these ranges and needn't reach their ends.
There are 8 independent parts, one for each index of `dp`. The reference program is written for one: setup_inputs(seed, part) draws one part's arguments, and reference() takes and returns one part's arrays. A program takes and returns all parts, laid end to end along the dimension named above; an argument that names none is the same for every part. Nothing has to cross between parts.
Inputs may be any that keep to these rules, and one draw needn't show every extreme that they name: offsets[l, h] lies in 0 to 2**l - 1; at a level l with 2**l <= 16, each value 0 to 2**l - 1 is taken by exactly 16 / 2**l heads; at a level with 2**l > 16, the heads take the distinct values 0 to 15.
All inputs are finite; a program needn't handle non-finite values.
Results may differ from the reference program's by a relative error of at most 0.0055.
Values may be sent and summed in bfloat16 or wider, within the bound.
A program may use at most 128 MiB of HBM per device.

```python
import math
import jax
import jax.numpy as jnp
from jax import lax

D = 768
HEADS = 16
LEVELS = 5
TOK_DEV = 512
TOKENS = 16384


def shared_base(key):
    return jnp.clip(jax.random.normal(key, (TOKENS, D), jnp.float32), -6.0, 6.0)


def draw_keys(key, part):
    base = shared_base(key)
    return base.astype(jnp.bfloat16)


def draw_queries(key, part):
    key = jax.random.fold_in(key, 7)
    noise = jnp.clip(jax.random.normal(key, (TOKENS, D), jnp.float32), -6.0, 6.0)
    return noise.astype(jnp.bfloat16)


def draw_offsets(key, part):
    key = jax.random.fold_in(key, 5)
    levels_rows = []
    for level in range(LEVELS):
        order = jax.random.permutation(jax.random.fold_in(key, level), HEADS)
        levels_rows.append(order.astype(jnp.int32) % 2 ** level)
    return jnp.stack(levels_rows)


def block_scale(own_key, dims, cuts, smallest, largest):
    level = 1.0
    for axis_at, blocks in cuts:
        steps = jax.random.uniform(jax.random.fold_in(jax.random.fold_in(own_key, 6), axis_at), (blocks,), jnp.float32, smallest / len(cuts), largest / len(cuts))
        level = level * jnp.repeat(jnp.exp(steps), dims[axis_at] // blocks).reshape((-1,) + (1,) * (len(dims) - 1 - axis_at))
    return level


def centred(stream_key, shape, spread, reach, cuts=(), kind=jnp.bfloat16):
    gain = block_scale(stream_key, shape, cuts, -0.22, 0.18) if cuts else 1.0
    entries = jax.random.normal(stream_key, shape, jnp.float32) * spread * gain
    return jnp.minimum(jnp.maximum(entries, -reach), reach).astype(kind)


def setup_inputs(seed: int = 0, part: int = 0) -> dict:
    seeds = jax.random.split(jax.random.key(seed), 6)
    part_splits = jax.random.split(jax.random.fold_in(seeds[5], part), 6)
    queries = draw_queries(jax.random.fold_in(jax.random.fold_in(seeds[5], part), 71), part)
    keys = draw_keys(jax.random.fold_in(jax.random.fold_in(seeds[5], part), 71), part)
    values = centred(part_splits[2], (TOKENS, D), 1.0, 6.0, ((0, 32),))
    offsets = draw_offsets(jax.random.fold_in(seeds[5], 71), part)
    out_weight = centred(seeds[4], (D, D), D ** -0.5, 0.21875)
    return {"queries": queries, "keys": keys, "values": values, "offsets": offsets, "out_weight": out_weight}


def reference(queries, keys, values, offsets, out_weight):
    head_dim = D // HEADS
    scale = 1.0 / math.sqrt(head_dim)
    q_heads = queries.reshape(TOKENS, HEADS, head_dim).transpose(1, 0, 2)
    k_heads = keys.reshape(TOKENS, HEADS, head_dim).transpose(1, 0, 2)
    v_heads = values.reshape(TOKENS, HEADS, head_dim).transpose(1, 0, 2)

    def per_head(inputs):
        q_one, k_one, v_one, head_offsets = inputs
        level_outs = []
        level_lses = []
        for level in range(LEVELS):
            ratio = 2 ** level
            if level == LEVELS - 1:
                seg_len = TOKENS
            else:
                seg_len = TOK_DEV * ratio
            segments = TOKENS // seg_len
            kept = seg_len // ratio
            offset = head_offsets[level].astype(jnp.int32)

            def pick(x):
                grouped = x.reshape(segments, kept, ratio, head_dim)
                return lax.dynamic_index_in_dim(grouped, offset, axis=2, keepdims=False)
            q_kept = pick(q_one).astype(jnp.float32)
            k_kept = pick(k_one).astype(jnp.float32)
            v_kept = pick(v_one).astype(jnp.float32)
            scores = jnp.einsum('smd,snd->smn', q_kept, k_kept) * scale
            top = lax.optimization_barrier(jnp.max(scores, axis=-1))
            weights = jnp.exp(scores - top[..., None])
            total = lax.optimization_barrier(jnp.sum(weights, axis=-1))
            rounded = lax.optimization_barrier(weights.astype(jnp.bfloat16)).astype(jnp.float32)
            level_out = jnp.einsum('smn,snd->smd', rounded, v_kept) / total[..., None]
            level_lse = top + jnp.log(total)
            lanes = jnp.arange(ratio, dtype=jnp.int32) == offset
            full_out = (level_out[:, :, None, :] * lanes.astype(jnp.float32)[None, None, :, None]).reshape(TOKENS, head_dim)
            full_lse = jnp.where(lanes[None, None, :], level_lse[:, :, None], jnp.float32(-1e+30)).reshape(TOKENS)
            level_outs.append(full_out)
            level_lses.append(full_lse)
        lse_all = jnp.stack(level_lses)
        out_all = jnp.stack(level_outs)
        peak = lax.optimization_barrier(jnp.max(lse_all, axis=0))
        shares = jnp.exp(lse_all - peak[None])
        return lax.optimization_barrier(jnp.sum(shares[..., None] * out_all, axis=0)) / lax.optimization_barrier(jnp.sum(shares, axis=0))[:, None]
    merged = lax.map(per_head, (q_heads, k_heads, v_heads, offsets.T))
    merged = merged.transpose(1, 0, 2).reshape(TOKENS, D).astype(jnp.bfloat16)
    return jnp.dot(merged, out_weight, preferred_element_type=jnp.float32).astype(jnp.bfloat16)
```

```python
import math

import jax
import jax.numpy as jnp
from jax import lax
from jax.experimental import pallas as pl
from jax.experimental.pallas import tpu as pltpu
from jax.sharding import PartitionSpec as P

MESH = pl.DeviceIdType.MESH
BF = jnp.bfloat16
F32 = jnp.float32
ROWS = 512
WIDTH = 768
HALF = 384
HD = 48
NH = 8
COEF = math.log2(math.e) / math.sqrt(HD)
NT = (((1,), (1,)), ((), ()))
KEPT = [ROWS >> level for level in range(5)]


def reversed_bits(x, bits):
    out = jnp.zeros_like(x)
    for b in range(bits):
        out = out + ((x >> b) & 1) * (1 << (bits - 1 - b))
    return out


def window(first, count):
    lo, hi = HD * first, HD * (first + count)
    start = lo // 128 * 128
    width = 128 if hi <= start + 128 else 256
    return start, width


def head_mask(head, start, width):
    lane = lax.broadcasted_iota(jnp.int32, (1, width), 1) + start
    return (lane >= HD * head) & (lane < HD * head + HD)


def softmax_unit(q, k, v):
    s = lax.dot_general(q, k, NT, preferred_element_type=F32)
    top = jnp.max(s, axis=1, keepdims=True) * COEF
    p = jnp.exp2(s * COEF - top)
    total = jnp.sum(p, axis=1, keepdims=True)
    o = jnp.dot(p.astype(BF), v, preferred_element_type=F32)
    return o, top, total


def kernel(
    off_ref, q_ref, k_ref, v_ref, w_ref, out_ref,
    stage, halves, s1, s2, s3, c4, r2, r3, y4, q1, q2, q3, q4,
    acc0, acc1, acc2, acc3, acc4, top0, top1, top2, top3, top4,
    sum0, sum1, sum2, sum3, sum4, unperm, msend, mrecv, send_sem, recv_sem,
):
    me = lax.axis_index("seq")
    core = lax.rem(me, 2)
    z = lax.rem(me // 2, 4)
    y = me // 8

    def at(yy, zz, cc):
        return {"seq": (yy * 4 + zz) * 2 + cc}

    sibling = at(y, z, 1 - core)
    z_peers = [at(y, z + 1 - 2 * lax.rem(z, 2), core), at(y, lax.rem(z + 2, 4), core), at(y, 3 - z, core)]
    y_peers = [at(lax.rem(y + d, 4), z, core) for d in (1, 2, 3)]
    barrier = pltpu.get_barrier_semaphore()
    for peer in [sibling] + z_peers + y_peers:
        pl.semaphore_signal(barrier, inc=1, device_id=peer, device_id_type=MESH)

    def remote(slot, src, dst, peer):
        return pltpu.make_async_remote_copy(
            src_ref=src, dst_ref=dst, send_sem=send_sem.at[slot], recv_sem=recv_sem.at[slot],
            device_id=peer, device_id_type=MESH,
        )

    dest = lax.broadcasted_iota(jnp.int32, (ROWS, 1), 0)
    source = (dest & 31) * 16 + reversed_bits(dest >> 5, 4)
    lane512 = lax.broadcasted_iota(jnp.int32, (ROWS, ROWS), 1)
    perm = jnp.where(lane512 == source, 1.0, 0.0).astype(BF)
    mine = pl.ds(pl.multiple_of(core * HALF, 128), HALF)
    theirs = pl.ds(pl.multiple_of((1 - core) * HALF, 128), HALF)

    def permuted(ref, lanes):
        return jnp.dot(perm, ref[:, lanes], preferred_element_type=F32).astype(BF)

    stage[0] = permuted(k_ref, theirs)
    stage[1] = permuted(v_ref, theirs)
    pl.semaphore_wait(barrier, 7)
    kv_copy = remote(0, stage.at[pl.ds(0, 2)], halves.at[1, pl.ds(0, 2)], sibling)
    kv_copy.start()
    stage[2] = permuted(q_ref, theirs)
    q_copy = remote(1, stage.at[2], halves.at[1, 2], sibling)
    q_copy.start()
    halves[0, 0] = permuted(k_ref, mine)
    halves[0, 1] = permuted(v_ref, mine)

    offs = off_ref[...].astype(BF)
    head_row = lax.broadcasted_iota(jnp.int32, (16, HALF), 0)
    head_col = lax.broadcasted_iota(jnp.int32, (16, HALF), 1) // HD + NH * core
    off_cols = jnp.dot(offs, jnp.where(head_row == head_col, 1.0, 0.0).astype(BF), preferred_element_type=F32)
    stat_row = lax.broadcasted_iota(jnp.int32, (16, 128), 0)
    stat_col = (lax.broadcasted_iota(jnp.int32, (16, 128), 1) & 7) + NH * core
    off_stat = jnp.dot(offs, jnp.where(stat_row == stat_col, 1.0, 0.0).astype(BF), preferred_element_type=F32)
    block_cols, block_stat = [None], [None]
    for level in range(1, 5):
        block_cols.append(reversed_bits(off_cols[level:level + 1].astype(jnp.int32), level))
        block_stat.append(reversed_bits(off_stat[level:level + 1].astype(jnp.int32), level))

    def select(src, kind, level):
        n = KEPT[level]
        kept = halves[src, kind, 0:n]
        for b in range(1, 1 << level):
            kept = jnp.where(block_cols[level] == b, halves[src, kind, b * n:(b + 1) * n], kept)
        return kept

    c4_own = c4.at[0]
    for kind in range(2):
        c4[0, kind, 0:KEPT[4]] = select(0, kind, 4)
        s3[kind, 0:KEPT[3]] = select(0, kind, 3)
        s2[kind, 0:KEPT[2]] = select(0, kind, 2)
        s1[kind, 0:KEPT[1]] = select(0, kind, 1)
    kv_copy.wait_recv()
    for kind in range(2):
        c4[0, kind, KEPT[4]:] = select(1, kind, 4)
    z4 = [remote(2 + i, c4_own, c4.at[1 + i], z_peers[i]) for i in range(3)]
    for c in z4:
        c.start()
    for kind in range(2):
        s3[kind, KEPT[3]:] = select(1, kind, 3)
        s2[kind, KEPT[2]:] = select(1, kind, 2)
    z3 = [remote(5 + i, s3, r3.at[i], z_peers[i]) for i in range(3)]
    z2 = remote(8, s2, r2, z_peers[0])
    for kind in range(2):
        s1[kind, KEPT[1]:] = select(1, kind, 1)
    halves[0, 2] = permuted(q_ref, mine)
    q_copy.wait_recv()
    for src in range(2):
        q4[src * KEPT[4]:(src + 1) * KEPT[4]] = select(src, 2, 4)
        q3[src * KEPT[3]:(src + 1) * KEPT[3]] = select(src, 2, 3)
        q2[src * KEPT[2]:(src + 1) * KEPT[2]] = select(src, 2, 2)
        q1[src * KEPT[1]:(src + 1) * KEPT[1]] = select(src, 2, 1)

    stat_lane = lax.broadcasted_iota(jnp.int32, (1, 128), 1) & 7

    def attend(q_of, k_of, v_of, group, rows, acc, top_ref, sum_ref):
        tops = jnp.zeros((rows, 128), F32)
        sums = jnp.zeros((rows, 128), F32)
        written = set()
        for first in range(0, NH, group):
            start, width = window(first, group)
            masks = [head_mask(first + g, start, width) for g in range(group)]
            q = q_of(start, width)
            if group == 1:
                stack = q
                k = jnp.where(masks[0], k_of(start, width), jnp.zeros((), BF))
            else:
                stack = jnp.concatenate([jnp.where(m, q, jnp.zeros((), BF)) for m in masks], axis=0)
                k = k_of(start, width)
            o, top, total = softmax_unit(stack, k, v_of(start, width))
            for t in range(start, start + width, 128):
                part = None
                for g in range(group):
                    lo, hi = HD * (first + g), HD * (first + g + 1)
                    if hi <= t or lo >= t + 128:
                        continue
                    piece = o[g * rows:(g + 1) * rows, t - start:t - start + 128]
                    mask = masks[g][:, t - start:t - start + 128]
                    if part is None:
                        part = jnp.where(mask, piece, acc[:, t:t + 128]) if t in written else piece
                    else:
                        part = jnp.where(mask, piece, part)
                acc[:, t:t + 128] = part
                written.add(t)
            for g in range(group):
                lanes = stat_lane == first + g
                tops = jnp.where(lanes, top[g * rows:(g + 1) * rows], tops)
                sums = jnp.where(lanes, total[g * rows:(g + 1) * rows], sums)
        top_ref[...] = tops
        sum_ref[...] = sums

    def level0(s, carry):
        attend(
            lambda a, w: halves[s, 2, :, a:a + w],
            lambda a, w: halves[s, 0, :, a:a + w],
            lambda a, w: halves[s, 1, :, a:a + w],
            1, ROWS, acc0.at[s], top0.at[s], sum0.at[s],
        )
        return carry

    level0(0, 0)
    for c in z4:
        c.wait_recv()
    y4c = [remote(9 + i, c4, y4.at[i], y_peers[i]) for i in range(3)]
    for c in y4c:
        c.start()
    for c in z3:
        c.start()
    z2.start()
    level0(1, 0)
    attend(
        lambda a, w: q1[:, a:a + w], lambda a, w: s1[0, :, a:a + w], lambda a, w: s1[1, :, a:a + w],
        1, 2 * KEPT[1], acc1, top1, sum1,
    )
    dest2 = lax.broadcasted_iota(jnp.int32, (ROWS, 1), 0)
    back = reversed_bits(dest2 & 15, 4) * 32 + (dest2 >> 4)
    unperm[...] = jnp.where(lane512 == back, 1.0, 0.0).astype(BF)
    z2.wait_recv()

    def both2(kind):
        return lambda a, w: jnp.concatenate([s2[kind, :, a:a + w], r2[kind, :, a:a + w]], axis=0)

    attend(lambda a, w: q2[:, a:a + w], both2(0), both2(1), 2, 2 * KEPT[2], acc2, top2, sum2)
    for c in z3:
        c.wait_recv()

    def all3(kind):
        return lambda a, w: jnp.concatenate([s3[kind, :, a:a + w]] + [r3[i, kind, :, a:a + w] for i in range(3)], axis=0)

    attend(lambda a, w: q3[:, a:a + w], all3(0), all3(1), 4, 2 * KEPT[3], acc3, top3, sum3)
    for c in y4c:
        c.wait_recv()

    def all4(kind):
        return lambda a, w: jnp.concatenate(
            [c4[b, kind, :, a:a + w] for b in range(4)]
            + [y4[i, b, kind, :, a:a + w] for i in range(3) for b in range(4)], axis=0)

    attend(lambda a, w: q4[:, a:a + w], all4(0), all4(1), 4, 2 * KEPT[4], acc4, top4, sum4)

    spread_row = lax.broadcasted_iota(jnp.int32, (128, HALF), 0)
    spread_col = lax.broadcasted_iota(jnp.int32, (128, HALF), 1) // HD
    spread = jnp.where((spread_row < 16) & ((spread_row & 7) == spread_col), 1.0, 0.0).astype(BF)
    is_high = lax.broadcasted_iota(jnp.int32, (1, 128), 1) < 8
    row_class = lax.broadcasted_iota(jnp.int32, (ROWS, 1), 0) >> 5
    accs = [acc0, acc1, acc2, acc3, acc4]
    tops = [top0, top1, top2, top3, top4]
    sums = [sum0, sum1, sum2, sum3, sum4]

    def merge(s):
        def full(refs, level):
            if level == 0:
                return refs[0][s]
            n = KEPT[level]
            part = refs[level][s * n:(s + 1) * n]
            return jnp.concatenate([part] * (1 << level), axis=0)

        level_tops = [full(tops, 0)]
        for level in range(1, 5):
            match = (row_class >> (4 - level)) == block_stat[level]
            level_tops.append(jnp.where(match, full(tops, level), -1e30))
        peak = level_tops[0]
        for t in level_tops[1:]:
            peak = jnp.maximum(peak, t)
        shares = [jnp.exp2(t - peak) for t in level_tops]
        den = shares[0] * full(sums, 0)
        for level in range(1, 5):
            den = den + shares[level] * full(sums, level)
        inv = 1.0 / den
        merged = None
        for level in range(5):
            weight = shares[level] * inv
            high = weight.astype(BF).astype(F32)
            packed = jnp.where(is_high, high, weight - high).astype(BF)
            wide = jnp.dot(packed, spread, preferred_element_type=F32)
            term = wide * full(accs, level)
            merged = term if merged is None else merged + term
        return jnp.dot(unperm[...], merged.astype(BF), preferred_element_type=F32).astype(BF)

    msend[...] = merge(1)
    m_copy = remote(12, msend, mrecv, sibling)
    m_copy.start()
    own = merge(0)
    w_mine = w_ref[pl.ds(pl.multiple_of(core * HALF, 128), HALF), :]
    w_theirs = w_ref[pl.ds(pl.multiple_of((1 - core) * HALF, 128), HALF), :]
    projected = jnp.dot(own, w_mine, preferred_element_type=F32)
    m_copy.wait_recv()
    projected = projected + jnp.dot(mrecv[...], w_theirs, preferred_element_type=F32)
    out_ref[...] = projected.astype(BF)
    for c in [kv_copy, q_copy] + z4 + z3 + [z2] + y4c + [m_copy]:
        c.wait_send()


def body(queries, keys, values, offsets, out_weight):
    vmem = pl.BlockSpec(memory_space=pltpu.VMEM)
    n = KEPT
    scratch = [
        pltpu.VMEM((3, ROWS, HALF), BF),
        pltpu.VMEM((2, 3, ROWS, HALF), BF),
        pltpu.VMEM((2, 2 * n[1], HALF), BF),
        pltpu.VMEM((2, 2 * n[2], HALF), BF),
        pltpu.VMEM((2, 2 * n[3], HALF), BF),
        pltpu.VMEM((4, 2, 2 * n[4], HALF), BF),
        pltpu.VMEM((2, 2 * n[2], HALF), BF),
        pltpu.VMEM((3, 2, 2 * n[3], HALF), BF),
        pltpu.VMEM((3, 4, 2, 2 * n[4], HALF), BF),
    ]
    scratch += [pltpu.VMEM((2 * n[level], HALF), BF) for level in range(1, 5)]
    scratch += [pltpu.VMEM((2, ROWS, HALF), F32)]
    scratch += [pltpu.VMEM((2 * n[level], HALF), F32) for level in range(1, 5)]
    for _ in range(2):
        scratch += [pltpu.VMEM((2, ROWS, 128), F32)]
        scratch += [pltpu.VMEM((2 * n[level], 128), F32) for level in range(1, 5)]
    scratch += [
        pltpu.VMEM((ROWS, ROWS), BF),
        pltpu.VMEM((ROWS, HALF), BF),
        pltpu.VMEM((ROWS, HALF), BF),
        pltpu.SemaphoreType.DMA((13,)),
        pltpu.SemaphoreType.DMA((13,)),
    ]
    return pl.pallas_call(
        kernel,
        out_shape=jax.ShapeDtypeStruct((ROWS, WIDTH), BF),
        in_specs=[vmem] * 5,
        out_specs=vmem,
        scratch_shapes=scratch,
        compiler_params=pltpu.CompilerParams(collective_id=0, has_side_effects=True, vmem_limit_bytes=56 << 20),
        cost_estimate=pl.CostEstimate(flops=3 * 10**9, bytes_accessed=5 * 10**6, transcendentals=9 * 10**6),
        name="dilated_attention",
    )(offsets, queries, keys, values, out_weight)


def solution(mesh):
    return jax.shard_map(
        body,
        mesh=mesh,
        in_specs=(P(("dp", "seq"), None), P(("dp", "seq"), None), P(("dp", "seq"), None), P(), P()),
        out_specs=P(("dp", "seq"), None),
        check_vma=False,
    )
```

```python
import math

import jax
import jax.numpy as jnp
from jax import lax
from jax.experimental import pallas as pl
from jax.experimental.pallas import tpu as pltpu
from jax.sharding import PartitionSpec as P

MESH = pl.DeviceIdType.MESH
BF = jnp.bfloat16
F32 = jnp.float32
ROWS = 512
WIDTH = 768
HALF = 384
HD = 48
NH = 8
COEF = math.log2(math.e) / math.sqrt(HD)
NT = (((1,), (1,)), ((), ()))
KEPT = [ROWS >> level for level in range(5)]


def reversed_bits(x, bits):
    out = jnp.zeros_like(x)
    for b in range(bits):
        out = out + ((x >> b) & 1) * (1 << (bits - 1 - b))
    return out


def window(first, count):
    lo, hi = HD * first, HD * (first + count)
    start = lo // 128 * 128
    width = 128 if hi <= start + 128 else 256
    return start, width


def head_mask(head, start, width):
    lane = lax.broadcasted_iota(jnp.int32, (1, width), 1) + start
    return (lane >= HD * head) & (lane < HD * head + HD)


def softmax_unit(q, k, v):
    s = lax.dot_general(q, k, NT, preferred_element_type=F32)
    top = jnp.max(s, axis=1, keepdims=True) * COEF
    p = jnp.exp2(s * COEF - top)
    total = jnp.sum(p, axis=1, keepdims=True)
    o = jnp.dot(p.astype(BF), v, preferred_element_type=F32)
    return o, top, total


def kernel(
    off_ref, q_hbm, k_hbm, v_hbm, out_hbm,
    q_ref, k_ref, v_ref, stage, halves, s1, s2, s3, c4, r2, r3, q1, q2, q3, qy,
    acc0, acc1, acc2, acc3, acc4, top0, top1, top2, top3, top4,
    sum0, sum1, sum2, sum3, sum4, o3, t3, u3, o3_out, o3_in, st3_out, st3_in, st4_out, acc4_in, st4_in, m4, t4, u4,
    unperm, msend, local_sem, send_sem, recv_sem,
):
    me = lax.axis_index("seq")
    core = lax.rem(me, 2)
    z = lax.rem(me // 2, 4)
    y = me // 8

    loads = [
        pltpu.make_async_copy(src, dst, local_sem.at[i])
        for i, (src, dst) in enumerate([(k_hbm, k_ref), (v_hbm, v_ref), (q_hbm, q_ref)])
    ]
    for c in loads:
        c.start()

    def at(yy, zz, cc):
        return {"seq": (yy * 4 + zz) * 2 + cc}

    sibling = at(y, z, 1 - core)
    pair = at(y, z + 1 - 2 * lax.rem(z, 2), core)
    mirror = at(y, 3 - z, core)
    mirror_pair = at(y, 3 - (z + 1 - 2 * lax.rem(z, 2)), core)
    y_next = [at(lax.rem(y + d, 4), z, core) for d in (1, 2, 3)]
    y_back = [at(lax.rem(y + 4 - d, 4), z, core) for d in (1, 2, 3)]
    is_centre = (z + 1) // 2 == 1
    barrier = pltpu.get_barrier_semaphore()
    for peer in [sibling, pair, mirror, mirror_pair] + y_next:
        pl.semaphore_signal(barrier, inc=1, device_id=peer, device_id_type=MESH)

    def remote(send, recv, src, dst, peer):
        return pltpu.make_async_remote_copy(
            src_ref=src, dst_ref=dst, send_sem=send_sem.at[send], recv_sem=recv_sem.at[recv],
            device_id=peer, device_id_type=MESH,
        )

    kv_copy = remote(0, 0, stage.at[pl.ds(0, 2)], halves.at[1, pl.ds(0, 2)], sibling)
    q_copy = remote(1, 1, stage.at[2], halves.at[1, 2], sibling)
    l4_pair = remote(2, 2, c4.at[0], c4.at[1], pair)
    l4_mirror = remote(3, 3, c4.at[0], c4.at[2], mirror)
    l4_cross = remote(4, 4, c4.at[0], c4.at[3], mirror_pair)
    l4_fwd_mirror = remote(22, 4, c4.at[1], c4.at[3], mirror)
    l4_fwd_cross = remote(23, 3, c4.at[1], c4.at[2], mirror_pair)
    l3_pair = remote(5, 5, s3, r3.at[0], pair)
    l3_mirror = remote(6, 6, s3, r3.at[1], mirror)
    l3_fwd = remote(7, 7, r3.at[0], r3.at[2], mirror)
    n3 = 2 * KEPT[3]
    l3_q = remote(8, 8, q3.at[pl.ds(0, n3)], q3.at[pl.ds(n3, n3)], pair)
    l3_out = remote(9, 9, o3_out, o3_in, pair)
    l3_stat = remote(10, 10, st3_out, st3_in, pair)
    l2_copy = remote(11, 11, s2, r2, pair)
    n4 = 2 * KEPT[4]
    y_q = [remote(12 + i, 12 + i, qy.at[0], qy.at[i + 1], y_next[i]) for i in range(3)]
    y_acc = [remote(15 + i, 15 + i, acc4.at[pl.ds((i + 1) * n4, n4)], acc4_in.at[i], y_back[i]) for i in range(3)]
    y_stat = [remote(18 + i, 18 + i, st4_out.at[pl.ds((i + 1) * n4, n4)], st4_in.at[i], y_back[i]) for i in range(3)]

    dest = lax.broadcasted_iota(jnp.int32, (ROWS, 1), 0)
    source = (dest & 31) * 16 + reversed_bits(dest >> 5, 4)
    lane512 = lax.broadcasted_iota(jnp.int32, (ROWS, ROWS), 1)
    perm = jnp.where(lane512 == source, 1.0, 0.0).astype(BF)
    mine = pl.ds(pl.multiple_of(core * HALF, 128), HALF)
    theirs = pl.ds(pl.multiple_of((1 - core) * HALF, 128), HALF)

    def permuted(ref, lanes):
        return jnp.dot(perm, ref[:, lanes], preferred_element_type=F32).astype(BF)

    loads[0].wait()
    stage[0] = permuted(k_ref, theirs)
    loads[1].wait()
    stage[1] = permuted(v_ref, theirs)
    pl.semaphore_wait(barrier, 7)
    kv_copy.start()
    halves[0, 0] = permuted(k_ref, mine)
    halves[0, 1] = permuted(v_ref, mine)
    loads[2].wait()
    stage[2] = permuted(q_ref, theirs)
    q_copy.start()
    halves[0, 2] = permuted(q_ref, mine)

    offs = off_ref[...].astype(BF)
    head_row = lax.broadcasted_iota(jnp.int32, (16, HALF), 0)
    head_col = lax.broadcasted_iota(jnp.int32, (16, HALF), 1) // HD + NH * core
    off_cols = jnp.dot(offs, jnp.where(head_row == head_col, 1.0, 0.0).astype(BF), preferred_element_type=F32)
    stat_row = lax.broadcasted_iota(jnp.int32, (16, 128), 0)
    stat_col = (lax.broadcasted_iota(jnp.int32, (16, 128), 1) & 7) + NH * core
    off_stat = jnp.dot(offs, jnp.where(stat_row == stat_col, 1.0, 0.0).astype(BF), preferred_element_type=F32)
    block_cols, block_stat = [None], [None]
    for level in range(1, 5):
        block_cols.append(reversed_bits(off_cols[level:level + 1].astype(jnp.int32), level))
        block_stat.append(reversed_bits(off_stat[level:level + 1].astype(jnp.int32), level))

    def select(src, kind, level):
        n = KEPT[level]
        kept = halves[src, kind, 0:n]
        for b in range(1, 1 << level):
            kept = jnp.where(block_cols[level] == b, halves[src, kind, b * n:(b + 1) * n], kept)
        return kept

    for kind in range(2):
        c4[0, kind, 0:KEPT[4]] = select(0, kind, 4)
        s3[kind, 0:KEPT[3]] = select(0, kind, 3)
    q3[0:KEPT[3]] = select(0, 2, 3)
    qy[0, 0:KEPT[4]] = select(0, 2, 4)
    kv_copy.wait_recv()
    for kind in range(2):
        c4[0, kind, KEPT[4]:] = select(1, kind, 4)
    l4_pair.start()

    @pl.when(is_centre)
    def _():
        l4_mirror.start()
        l4_cross.start()

    for kind in range(2):
        s3[kind, KEPT[3]:] = select(1, kind, 3)

    @pl.when(is_centre)
    def _():
        l3_mirror.start()

    @pl.when(jnp.logical_not(is_centre))
    def _():
        l3_pair.start()

    q_copy.wait_recv()
    q3[KEPT[3]:2 * KEPT[3]] = select(1, 2, 3)
    qy[0, KEPT[4]:] = select(1, 2, 4)
    for c in y_q:
        c.start()

    @pl.when(jnp.logical_not(is_centre))
    def _():
        l3_q.start()

    for src in range(2):
        for kind in range(2):
            s2[kind, src * KEPT[2]:(src + 1) * KEPT[2]] = select(src, kind, 2)

    stat_lane = lax.broadcasted_iota(jnp.int32, (1, 128), 1) & 7

    def attend(q_of, k_of, v_of, group, rows, acc, top_ref, sum_ref, heads=(0, NH), norm=False):
        tops = jnp.zeros((rows, 128), F32) if heads[0] == 0 else top_ref[...]
        sums = jnp.zeros((rows, 128), F32) if heads[0] == 0 else sum_ref[...]
        written = {t for t in range(0, HALF, 128) if t < HD * heads[0]}
        for first in range(heads[0], heads[1], group):
            start, width = window(first, group)
            masks = [head_mask(first + g, start, width) for g in range(group)]
            q = q_of(start, width)
            if group == 1:
                stack = q
                k = jnp.where(masks[0], k_of(start, width), jnp.zeros((), BF))
            else:
                stack = jnp.concatenate([jnp.where(m, q, jnp.zeros((), BF)) for m in masks], axis=0)
                k = k_of(start, width)
            o, top, total = softmax_unit(stack, k, v_of(start, width))
            if norm:
                o = o * (1.0 / total)
            for t in range(start, start + width, 128):
                part = None
                for g in range(group):
                    lo, hi = HD * (first + g), HD * (first + g + 1)
                    if hi <= t or lo >= t + 128:
                        continue
                    piece = o[g * rows:(g + 1) * rows, t - start:t - start + 128]
                    mask = masks[g][:, t - start:t - start + 128]
                    if part is None:
                        part = jnp.where(mask, piece, acc[:, t:t + 128]) if t in written else piece
                    else:
                        part = jnp.where(mask, piece, part)
                acc[:, t:t + 128] = part
                written.add(t)
            for g in range(group):
                lanes = stat_lane == first + g
                tops = jnp.where(lanes, top[g * rows:(g + 1) * rows], tops)
                sums = jnp.where(lanes, total[g * rows:(g + 1) * rows], sums)
        top_ref[...] = tops
        sum_ref[...] = sums

    def level0(s, heads):
        attend(
            lambda a, w: halves[s, 2, :, a:a + w],
            lambda a, w: halves[s, 0, :, a:a + w],
            lambda a, w: halves[s, 1, :, a:a + w],
            1, ROWS, acc0.at[s], top0.at[s], sum0.at[s], heads,
        )

    level0(0, (0, 4))

    @pl.when(is_centre)
    def _():
        l4_pair.wait_recv()
        l4_fwd_mirror.start()
        l4_fwd_cross.start()

    level0(0, (4, 8))

    @pl.when(is_centre)
    def _():
        l3_pair.wait_recv()
        l3_fwd.start()

    l2_copy.start()
    for src in range(2):
        q2[src * KEPT[2]:(src + 1) * KEPT[2]] = select(src, 2, 2)
        q1[src * KEPT[1]:(src + 1) * KEPT[1]] = select(src, 2, 1)
        for kind in range(2):
            s1[kind, src * KEPT[1]:(src + 1) * KEPT[1]] = select(src, kind, 1)
    level0(1, (0, 8))

    @pl.when(jnp.logical_not(is_centre))
    def _():
        l4_pair.wait_recv()

    l4_mirror.wait_recv()
    l4_cross.wait_recv()
    for c in y_q:
        c.wait_recv()

    def line4(kind):
        return lambda a, w: jnp.concatenate([c4[b, kind, :, a:a + w] for b in range(4)], axis=0)

    attend(
        lambda a, w: jnp.concatenate([qy[b, :, a:a + w] for b in range(4)], axis=0),
        line4(0), line4(1), 2, 4 * n4, acc4, top4, sum4,
    )
    stat_all = lax.broadcasted_iota(jnp.int32, (1, 128), 1)
    st4_out[...] = jnp.where(stat_all < 64, top4[...], sum4[...])
    for c in y_acc + y_stat:
        c.start()
    attend(
        lambda a, w: q1[:, a:a + w], lambda a, w: s1[0, :, a:a + w], lambda a, w: s1[1, :, a:a + w],
        1, 2 * KEPT[1], acc1, top1, sum1,
    )
    back = reversed_bits(dest & 15, 4) * 32 + (dest >> 4)
    unperm[...] = jnp.where(lane512 == back, 1.0, 0.0).astype(BF)

    @pl.when(is_centre)
    def _():
        l3_mirror.wait_recv()
        l3_fwd.wait_recv()
        l3_q.wait_recv()

        def all3(kind):
            return lambda a, w: jnp.concatenate(
                [s3[kind, :, a:a + w]] + [r3[i, kind, :, a:a + w] for i in range(3)], axis=0)

        attend(lambda a, w: q3[:, a:a + w], all3(0), all3(1), 2, 2 * n3, acc3, top3, sum3, norm=True)
        o3_out[...] = acc3[n3:].astype(BF)
        st3_out[...] = jnp.where(stat_all < 16, top3[n3:], sum3[n3:]).T[0:32]
        l3_out.start()
        l3_stat.start()
        o3[...] = acc3[0:n3].astype(BF)
        t3[...] = top3[0:n3]
        u3[...] = sum3[0:n3]

    l2_copy.wait_recv()

    def both2(kind):
        return lambda a, w: jnp.concatenate([s2[kind, :, a:a + w], r2[kind, :, a:a + w]], axis=0)

    attend(lambda a, w: q2[:, a:a + w], both2(0), both2(1), 2, 2 * KEPT[2], acc2, top2, sum2)

    spread_row = lax.broadcasted_iota(jnp.int32, (128, HALF), 0)
    spread_col = lax.broadcasted_iota(jnp.int32, (128, HALF), 1) // HD
    spread = jnp.where((spread_row < 16) & ((spread_row & 7) == spread_col), 1.0, 0.0).astype(BF)

    def widened(weight):
        high = weight.astype(BF).astype(F32)
        low = jnp.where(stat_all < 16, weight - high, 0.0)
        packed = jnp.where(stat_all < 8, high, low).astype(BF)
        return jnp.dot(packed, spread, preferred_element_type=F32)

    for c in y_acc + y_stat:
        c.wait_recv()
    tops4 = [top4[0:n4]] + [st4_in[i] for i in range(3)]
    sums4 = [sum4[0:n4]] + [pltpu.roll(st4_in[i], 64, 1) for i in range(3)]
    accs4 = [acc4[0:n4]] + [acc4_in[i] for i in range(3)]
    peak4 = jnp.maximum(jnp.maximum(tops4[0], tops4[1]), jnp.maximum(tops4[2], tops4[3]))
    parts4 = [jnp.exp2(t - peak4) for t in tops4]
    t4[...] = peak4
    u4[...] = parts4[0] * sums4[0] + parts4[1] * sums4[1] + parts4[2] * sums4[2] + parts4[3] * sums4[3]
    total4 = widened(parts4[0]) * accs4[0]
    for i in range(1, 4):
        total4 = total4 + widened(parts4[i]) * accs4[i]
    m4[...] = total4

    @pl.when(jnp.logical_not(is_centre))
    def _():
        l3_out.wait_recv()
        l3_stat.wait_recv()
        o3[...] = o3_in[...]
        zeros = jnp.zeros((112, 128), F32)
        t3[...] = jnp.concatenate([st3_in[0:16], zeros], axis=0).T
        u3[...] = jnp.concatenate([st3_in[16:32], zeros], axis=0).T

    row_class = lax.broadcasted_iota(jnp.int32, (ROWS, 1), 0) >> 5
    accs = [acc0, acc1, acc2, o3, m4]
    tops = [top0, top1, top2, t3, t4]
    sums = [sum0, sum1, sum2, u3, u4]

    def merge(s):
        def full(refs, level):
            if level == 0:
                return refs[0][s]
            n = KEPT[level]
            part = refs[level][s * n:(s + 1) * n]
            return jnp.concatenate([part] * (1 << level), axis=0)

        level_tops = [full(tops, 0)]
        for level in range(1, 5):
            match = (row_class >> (4 - level)) == block_stat[level]
            level_tops.append(jnp.where(match, full(tops, level), -1e30))
        peak = level_tops[0]
        for t in level_tops[1:]:
            peak = jnp.maximum(peak, t)
        shares = [jnp.exp2(t - peak) for t in level_tops]
        weighted = [shares[level] * full(sums, level) for level in range(5)]
        inv = 1.0 / (weighted[0] + weighted[1] + weighted[2] + weighted[3] + weighted[4])
        merged = None
        for level in range(5):
            term = widened((weighted if level == 3 else shares)[level] * inv) * full(accs, level).astype(F32)
            merged = term if merged is None else merged + term
        return jnp.dot(unperm[...], merged.astype(BF), preferred_element_type=F32).astype(BF)

    msend[1] = merge(1)
    m_copy = remote(21, 21, msend.at[1], out_hbm.at[:, mine], sibling)
    m_copy.start()
    msend[0] = merge(0)
    store = pltpu.make_async_copy(msend.at[0], out_hbm.at[:, mine], local_sem.at[3])
    store.start()

    @pl.when(is_centre)
    def _():
        for c in [l4_mirror, l4_cross, l4_fwd_mirror, l4_fwd_cross, l3_mirror, l3_fwd, l3_out, l3_stat]:
            c.wait_send()

    @pl.when(jnp.logical_not(is_centre))
    def _():
        for c in [l3_pair, l3_q]:
            c.wait_send()

    for c in [kv_copy, q_copy, l4_pair, l2_copy] + y_q + y_acc + y_stat:
        c.wait_send()
    store.wait()
    m_copy.wait()


def body(queries, keys, values, offsets, out_weight):
    n = [2 * k for k in KEPT]
    bf = [
        (ROWS, WIDTH), (ROWS, WIDTH), (ROWS, WIDTH), (3, ROWS, HALF), (2, 3, ROWS, HALF),
        (2, n[1], HALF), (2, n[2], HALF), (2, n[3], HALF), (4, 2, n[4], HALF), (2, n[2], HALF), (3, 2, n[3], HALF),
        (n[1], HALF), (n[2], HALF), (2 * n[3], HALF), (4, n[4], HALF),
    ]
    scratch = [pltpu.VMEM(shape, BF) for shape in bf]
    for width in (HALF, 128, 128):
        scratch += [pltpu.VMEM(shape, F32) for shape in [
            (2, ROWS, width), (n[1], width), (n[2], width), (2 * n[3], width), (4 * n[4], width)]]
    scratch += [
        pltpu.VMEM((n[3], HALF), BF), pltpu.VMEM((n[3], 128), F32), pltpu.VMEM((n[3], 128), F32),
        pltpu.VMEM((n[3], HALF), BF), pltpu.VMEM((n[3], HALF), BF),
        pltpu.VMEM((32, 128), F32), pltpu.VMEM((32, 128), F32),
        pltpu.VMEM((4 * n[4], 128), F32), pltpu.VMEM((3, n[4], HALF), F32), pltpu.VMEM((3, n[4], 128), F32),
        pltpu.VMEM((n[4], HALF), F32), pltpu.VMEM((n[4], 128), F32), pltpu.VMEM((n[4], 128), F32),
        pltpu.VMEM((ROWS, ROWS), BF),
        pltpu.VMEM((2, ROWS, HALF), BF),
        pltpu.SemaphoreType.DMA((4,)),
        pltpu.SemaphoreType.DMA((24,)),
        pltpu.SemaphoreType.DMA((24,)),
    ]
    merged = pl.pallas_call(
        kernel,
        out_shape=jax.ShapeDtypeStruct((ROWS, WIDTH), BF),
        in_specs=[pl.BlockSpec(memory_space=pltpu.VMEM)] + [pl.BlockSpec(memory_space=pl.ANY)] * 3,
        out_specs=pl.BlockSpec(memory_space=pl.ANY),
        scratch_shapes=scratch,
        compiler_params=pltpu.CompilerParams(collective_id=0, has_side_effects=True, vmem_limit_bytes=56 << 20),
        cost_estimate=pl.CostEstimate(flops=3 * 10**9, bytes_accessed=5 * 10**6, transcendentals=9 * 10**6),
        name="dilated_attention",
    )(offsets, queries, keys, values)
    return jnp.dot(merged, out_weight, preferred_element_type=F32).astype(BF)


def solution(mesh):
    return jax.shard_map(
        body,
        mesh=mesh,
        in_specs=(P(("dp", "seq"), None), P(("dp", "seq"), None), P(("dp", "seq"), None), P(), P()),
        out_specs=P(("dp", "seq"), None),
        check_vma=False,
    )
```

```python
import math

import jax
import jax.numpy as jnp
from jax import lax
from jax.experimental import pallas as pl
from jax.experimental.pallas import tpu as pltpu
from jax.sharding import PartitionSpec as P

MESH = pl.DeviceIdType.MESH
BF = jnp.bfloat16
F32 = jnp.float32
ROWS = 512
WIDTH = 768
HALF = 384
HD = 48
NH = 8
COEF = math.log2(math.e) / math.sqrt(HD)
NT = (((1,), (1,)), ((), ()))
KEPT = [ROWS >> level for level in range(5)]


def reversed_bits(x, bits):
    out = jnp.zeros_like(x)
    for b in range(bits):
        out = out + ((x >> b) & 1) * (1 << (bits - 1 - b))
    return out


def window(first, count):
    lo, hi = HD * first, HD * (first + count)
    start = lo // 128 * 128
    width = 128 if hi <= start + 128 else 256
    return start, width


def head_mask(head, start, width):
    lane = lax.broadcasted_iota(jnp.int32, (1, width), 1) + start
    return (lane >= HD * head) & (lane < HD * head + HD)


def softmax_unit(q, k, v):
    s = lax.dot_general(q, k, NT, preferred_element_type=F32)
    top = jnp.max(s, axis=1, keepdims=True) * COEF
    p = jnp.exp2(s * COEF - top)
    total = jnp.sum(p, axis=1, keepdims=True)
    o = jnp.dot(p.astype(BF), v, preferred_element_type=F32)
    return o, top, total


def kernel(
    off_hbm, q_hbm, k_hbm, v_hbm, out_ref,
    off_ref, q_ref, k_ref, v_ref, stage, halves, s1, c2, c3, c4, x2, x3, x4, q1, q2, q3, qy,
    acc0, acc1, acc2, acc3, acc4, top0, top1, top2, top3, top4,
    sum0, sum1, sum2, sum3, sum4, o3, t3, u3, o3_out, o3_in, st3_out, st3_in, acc4_out, st4_out, acc4_in, st4_in, m4, t4, u4,
    unperm, msend, local_sem, send_sem, recv_sem,
):
    me = lax.axis_index("seq")
    core = lax.rem(me, 2)
    z = lax.rem(me // 2, 4)
    y = me // 8

    loads = [
        pltpu.make_async_copy(src, dst, local_sem.at[i])
        for i, (src, dst) in enumerate([(k_hbm, k_ref), (v_hbm, v_ref), (q_hbm, q_ref), (off_hbm, off_ref)])
    ]
    for i in (3, 0, 1, 2):
        loads[i].start()

    def at(yy, zz, cc):
        return {"seq": (yy * 4 + zz) * 2 + cc}

    z_pair = z + 1 - 2 * lax.rem(z, 2)
    sibling = at(y, z, 1 - core)
    pair, pair_other = at(y, z_pair, core), at(y, z_pair, 1 - core)
    mirror, mirror_other = at(y, 3 - z, core), at(y, 3 - z, 1 - core)
    y_next = [at(lax.rem(y + d, 4), z, core) for d in (1, 2, 3)]
    y_back = [at(lax.rem(y + 4 - d, 4), z, core) for d in (1, 2, 3)]
    is_centre = (z + 1) // 2 == 1
    is_end = jnp.logical_not(is_centre)
    barrier = pltpu.get_barrier_semaphore()
    for peer in [sibling, pair, pair_other, mirror, mirror_other] + y_next:
        pl.semaphore_signal(barrier, inc=1, device_id=peer, device_id_type=MESH)

    def remote(send, recv, src, dst, peer):
        return pltpu.make_async_remote_copy(
            src_ref=src, dst_ref=dst, send_sem=send_sem.at[send], recv_sem=recv_sem.at[recv],
            device_id=peer, device_id_type=MESH,
        )

    kv_copy = remote(0, 0, stage.at[pl.ds(0, 2)], halves.at[1, pl.ds(0, 2)], sibling)
    q_copy = remote(1, 1, stage.at[2], halves.at[1, 2], sibling)
    def spread_out(first, slots, extra):
        return [
            remote(first, first, extra, slots.at[0, core], sibling),
            remote(first + 1, first + 1, slots.at[0, core], slots.at[1, core], pair),
            remote(first + 2, first + 2, extra, slots.at[1, core], pair_other),
        ]

    def to_mirror(first, slots, extra):
        return [
            remote(first, first, slots.at[0, core], slots.at[2, core], mirror),
            remote(first + 1, first + 1, extra, slots.at[2, core], mirror_other),
        ]

    l4_sib, *l4_pair = spread_out(2, c4, x4)
    l3_sib, *l3_pair = spread_out(5, c3, x3)
    l2_sib = remote(8, 8, x2, c2.at[0, core], sibling)
    l2_pair = []
    for t in range(3):
        tile = pl.ds(128 * t, 128)
        l2_pair += [
            remote(9 + 2 * t, 9 + 2 * t, c2.at[0, core, :, :, tile], c2.at[1, core, :, :, tile], pair),
            remote(10 + 2 * t, 10 + 2 * t, x2.at[:, :, tile], c2.at[1, core, :, :, tile], pair_other),
        ]
    l4_mirror = to_mirror(15, c4, x4)
    l3_mirror = to_mirror(17, c3, x3)
    l4_fwd_mirror = remote(19, 19, c4.at[1], c4.at[3], mirror)
    l4_fwd_pair2 = remote(20, 19, c4.at[2], c4.at[3], pair)
    l4_fwd_pair3 = remote(21, 20, c4.at[3], c4.at[2], pair)
    l3_fwd = remote(22, 21, c3.at[1], c3.at[3], mirror)
    n3 = 2 * KEPT[3]
    l3_q = remote(23, 22, q3.at[pl.ds(0, n3)], q3.at[pl.ds(n3, n3)], pair)
    l3_out = remote(24, 23, o3_out, o3_in, pair)
    l3_stat = remote(25, 24, st3_out, st3_in, pair)
    n4 = 2 * KEPT[4]
    y_q = [remote(26 + i, 26 + i, qy.at[0], qy.at[i + 1], y_next[i]) for i in range(3)]
    y_acc = [remote(29 + i, 29 + i, acc4_out.at[pl.ds(i * n4, n4)], acc4_in.at[i], y_back[i]) for i in range(3)]
    y_stat = [remote(32 + i, 32 + i, st4_out.at[(i + 1) // 2], st4_in.at[i], y_back[i]) for i in range(3)]
    m_copy = remote(35, 35, msend, out_ref.at[:, pl.ds(pl.multiple_of(core * HALF, 128), HALF)], sibling)

    dest = lax.broadcasted_iota(jnp.int32, (ROWS, 1), 0)
    source = (dest & 31) * 16 + reversed_bits(dest >> 5, 4)
    lane512 = lax.broadcasted_iota(jnp.int32, (ROWS, ROWS), 1)
    perm = jnp.where(lane512 == source, 1.0, 0.0).astype(BF)
    mine = pl.ds(pl.multiple_of(core * HALF, 128), HALF)
    theirs = pl.ds(pl.multiple_of((1 - core) * HALF, 128), HALF)

    def permuted(ref, lanes):
        return jnp.dot(perm, ref[:, lanes], preferred_element_type=F32).astype(BF)

    loads[3].wait()
    offs = off_ref[...].astype(BF)

    def reversed_offsets(heads):
        row = lax.broadcasted_iota(jnp.int32, heads.shape, 0)
        spread = jnp.dot(offs, jnp.where(row == heads, 1.0, 0.0).astype(BF), preferred_element_type=F32)
        return [None] + [reversed_bits(spread[level:level + 1].astype(jnp.int32), level) for level in range(1, 5)]

    column = lax.broadcasted_iota(jnp.int32, (16, HALF), 1) // HD
    mine_cols = reversed_offsets(column + NH * core)
    theirs_cols = reversed_offsets(column + NH * (1 - core))
    block_stat = reversed_offsets((lax.broadcasted_iota(jnp.int32, (16, 128), 1) & 7) + NH * core)

    def select(block, cols, level):
        n = KEPT[level]
        kept = block[0:n]
        for b in range(1, 1 << level):
            kept = jnp.where(cols[level] == b, block[b * n:(b + 1) * n], kept)
        return kept

    for kind, ref in enumerate([k_ref, v_ref]):
        loads[kind].wait()
        halves[0, kind] = permuted(ref, mine)
        stage[kind] = permuted(ref, theirs)
        c4[0, core, kind] = select(halves.at[0, kind], mine_cols, 4)
        x4[kind] = select(stage.at[kind], theirs_cols, 4)
    pl.semaphore_wait(barrier, 8)
    for c in l4_pair:
        c.start()

    @pl.when(is_centre)
    def _():
        for c in l4_mirror:
            c.start()

    for kind in range(2):
        c3[0, core, kind] = select(halves.at[0, kind], mine_cols, 3)
        x3[kind] = select(stage.at[kind], theirs_cols, 3)

    @pl.when(is_centre)
    def _():
        for c in l3_mirror:
            c.start()

    @pl.when(is_end)
    def _():
        for c in l3_pair:
            c.start()

    l4_sib.start()
    l3_sib.start()
    kv_copy.start()
    loads[2].wait()
    stage[2] = permuted(q_ref, theirs)
    q_copy.start()
    for kind in range(2):
        c2[0, core, kind] = select(halves.at[0, kind], mine_cols, 2)
        x2[kind] = select(stage.at[kind], theirs_cols, 2)

    @pl.when(is_centre)
    def _():
        for c in l2_pair:
            c.start()

    l2_sib.start()
    halves[0, 2] = permuted(q_ref, mine)
    for src in range(2):
        if src == 1:
            q_copy.wait_recv()
        block = halves.at[src, 2]
        qy[0, src * KEPT[4]:(src + 1) * KEPT[4]] = select(block, mine_cols, 4)
        q3[src * KEPT[3]:(src + 1) * KEPT[3]] = select(block, mine_cols, 3)
    for c in y_q:
        c.start()

    @pl.when(is_end)
    def _():
        l3_q.start()

    stat_lane = lax.broadcasted_iota(jnp.int32, (1, 128), 1) & 7

    def attend(q_of, k_of, v_of, group, rows, acc, top_ref, sum_ref, heads=(0, NH), norm=False):
        tops = jnp.zeros((rows, 128), F32) if heads[0] == 0 else top_ref[...]
        sums = jnp.zeros((rows, 128), F32) if heads[0] == 0 else sum_ref[...]
        written = {t for t in range(0, HALF, 128) if t < HD * heads[0]}
        for first in range(heads[0], heads[1], group):
            start, width = window(first, group)
            masks = [head_mask(first + g, start, width) for g in range(group)]
            q = q_of(start, width)
            if group == 1:
                stack = q
                k = jnp.where(masks[0], k_of(start, width), jnp.zeros((), BF))
            else:
                stack = jnp.concatenate([jnp.where(m, q, jnp.zeros((), BF)) for m in masks], axis=0)
                k = k_of(start, width)
            o, top, total = softmax_unit(stack, k, v_of(start, width))
            if norm:
                o = o * (1.0 / total)
            for t in range(start, start + width, 128):
                part = None
                for g in range(group):
                    lo, hi = HD * (first + g), HD * (first + g + 1)
                    if hi <= t or lo >= t + 128:
                        continue
                    piece = o[g * rows:(g + 1) * rows, t - start:t - start + 128]
                    mask = masks[g][:, t - start:t - start + 128]
                    if part is None:
                        part = jnp.where(mask, piece, acc[:, t:t + 128]) if t in written else piece
                    else:
                        part = jnp.where(mask, piece, part)
                acc[:, t:t + 128] = part
                written.add(t)
            for g in range(group):
                lanes = stat_lane == first + g
                tops = jnp.where(lanes, top[g * rows:(g + 1) * rows], tops)
                sums = jnp.where(lanes, total[g * rows:(g + 1) * rows], sums)
        top_ref[...] = tops
        sum_ref[...] = sums

    def level0(s, heads):
        attend(
            lambda a, w: halves[s, 2, :, a:a + w],
            lambda a, w: halves[s, 0, :, a:a + w],
            lambda a, w: halves[s, 1, :, a:a + w],
            1, ROWS, acc0.at[s], top0.at[s], sum0.at[s], heads,
        )

    level0(0, (0, 4))

    @pl.when(is_centre)
    def _():
        for c in l4_pair:
            c.wait_recv()
        l4_fwd_mirror.start()
        for c in l4_mirror:
            c.wait_recv()
        l4_fwd_pair2.start()

    level0(0, (4, NH))
    kv_copy.wait_recv()
    level0(1, (0, 4))

    @pl.when(is_centre)
    def _():
        for c in l3_pair:
            c.wait_recv()
        l3_fwd.start()
        l4_fwd_mirror.wait_recv()
        l4_fwd_pair3.start()

    @pl.when(is_end)
    def _():
        for c in l3_pair:
            c.wait_send()
        for c in l2_pair:
            c.start()

    level0(1, (4, NH))
    for src in range(2):
        q2[src * KEPT[2]:(src + 1) * KEPT[2]] = select(halves.at[src, 2], mine_cols, 2)
        q1[src * KEPT[1]:(src + 1) * KEPT[1]] = select(halves.at[src, 2], mine_cols, 1)
        for kind in range(2):
            s1[kind, src * KEPT[1]:(src + 1) * KEPT[1]] = select(halves.at[src, kind], mine_cols, 1)

    def level1(heads):
        attend(
            lambda a, w: q1[:, a:a + w], lambda a, w: s1[0, :, a:a + w], lambda a, w: s1[1, :, a:a + w],
            1, 2 * KEPT[1], acc1, top1, sum1, heads,
        )

    level1((0, 4))

    @pl.when(is_end)
    def _():
        for c in l4_pair:
            c.wait_recv()
        l4_fwd_pair2.wait_recv()
        l4_fwd_pair3.wait_recv()

    l4_sib.wait_recv()
    for c in y_q:
        c.wait_recv()

    def chips(ref, kind, slots):
        return lambda a, w: jnp.concatenate(
            [ref[slot, tok, kind, :, a:a + w] for slot in range(slots) for tok in range(2)], axis=0)

    attend(
        lambda a, w: jnp.concatenate([qy[b, :, a:a + w] for b in range(4)], axis=0),
        chips(c4, 0, 4), chips(c4, 1, 4), 2, 4 * n4, acc4, top4, sum4, norm=True,
    )
    stat_all = lax.broadcasted_iota(jnp.int32, (1, 128), 1)
    acc4_out[...] = acc4[n4:].astype(BF)
    packed4 = jnp.where(stat_all < 16, top4[...], sum4[...])
    for i in range(2):
        st4_out[i] = packed4[128 * i:128 * (i + 1)].T[0:32]
    for c in y_acc + y_stat:
        c.start()
    level1((4, NH))
    back = reversed_bits(dest & 15, 4) * 32 + (dest >> 4)
    unperm[...] = jnp.where(lane512 == back, 1.0, 0.0).astype(BF)

    l3_sib.wait_recv()

    @pl.when(is_centre)
    def _():
        for c in l3_mirror:
            c.wait_recv()
        l3_fwd.wait_recv()
        l3_q.wait_recv()
        attend(lambda a, w: q3[:, a:a + w], chips(c3, 0, 4), chips(c3, 1, 4), 2, 2 * n3, acc3, top3, sum3, norm=True)
        o3_out[...] = acc3[n3:].astype(BF)
        st3_out[...] = jnp.where(stat_all < 16, top3[n3:], sum3[n3:]).T[0:32]
        l3_out.start()
        l3_stat.start()
        o3[...] = acc3[0:n3].astype(BF)
        t3[...] = top3[0:n3]
        u3[...] = sum3[0:n3]

    row_class = lax.broadcasted_iota(jnp.int32, (ROWS, 1), 0) >> 5

    def full(ref, level, s):
        n = KEPT[level]
        return jnp.concatenate([ref[s * n:(s + 1) * n]] * (1 << level), axis=0)

    def full_top(ref, level, s):
        match = (row_class >> (4 - level)) == block_stat[level]
        return jnp.where(match, full(ref, level, s), -1e30)

    spread_row = lax.broadcasted_iota(jnp.int32, (128, HALF), 0)
    spread_col = lax.broadcasted_iota(jnp.int32, (128, HALF), 1) // HD
    spread = jnp.where((spread_row < 16) & ((spread_row & 7) == spread_col), 1.0, 0.0).astype(BF)

    def widened(weight):
        high = weight.astype(BF).astype(F32)
        low = jnp.where(stat_all < 16, weight - high, 0.0)
        packed = jnp.where(stat_all < 8, high, low).astype(BF)
        return jnp.dot(packed, spread, preferred_element_type=F32)

    for src in range(2):
        other = full_top(top1, 1, src)
        peak = jnp.maximum(top0[src], other)
        share0, share1 = jnp.exp2(top0[src] - peak), jnp.exp2(other - peak)
        top0[src] = peak
        sum0[src] = share0 * sum0[src] + share1 * full(sum1, 1, src)
        acc0[src] = widened(share0) * acc0[src] + widened(share1) * full(acc1, 1, src)

    l2_sib.wait_recv()
    for tile in range(3):
        for c in l2_pair[2 * tile:2 * tile + 2]:
            c.wait_recv()
        attend(
            lambda a, w: q2[:, a:a + w], chips(c2, 0, 2), chips(c2, 1, 2), 2, 2 * KEPT[2], acc2, top2, sum2,
            ((0, 2), (2, 4), (4, NH))[tile],
        )

    for c in y_acc + y_stat:
        c.wait_recv()
    zeros = jnp.zeros((112, 128), F32)

    def unpacked(stat):
        return [jnp.concatenate([stat[16 * i:16 * (i + 1)], zeros], axis=0).T for i in range(2)]

    tops4, sums4, accs4 = [top4[0:n4]], [sum4[0:n4]], [acc4[0:n4]]
    for i in range(3):
        at4 = (i + 1) % 2 * n4
        for part, stats in zip(unpacked(st4_in.at[i]), (tops4, sums4)):
            stats.append(part[at4:at4 + n4])
        accs4.append(acc4_in[i].astype(F32))
    peak4 = jnp.maximum(jnp.maximum(tops4[0], tops4[1]), jnp.maximum(tops4[2], tops4[3]))
    parts4 = [jnp.exp2(t - peak4) * total for t, total in zip(tops4, sums4)]
    t4[...] = peak4
    u4[...] = parts4[0] + parts4[1] + parts4[2] + parts4[3]
    total4 = widened(parts4[0]) * accs4[0]
    for i in range(1, 4):
        total4 = total4 + widened(parts4[i]) * accs4[i]
    m4[...] = total4

    @pl.when(is_end)
    def _():
        l3_out.wait_recv()
        l3_stat.wait_recv()
        o3[...] = o3_in[...]
        t3[...], u3[...] = unpacked(st3_in)

    rest = [(2, acc2, top2, sum2), (3, o3, t3, u3), (4, m4, t4, u4)]

    def merge(s):
        level_tops = [top0[s]] + [full_top(top, level, s) for level, _, top, _ in rest]
        peak = jnp.maximum(jnp.maximum(level_tops[0], level_tops[1]), jnp.maximum(level_tops[2], level_tops[3]))
        shares = [jnp.exp2(t - peak) for t in level_tops]
        weighted = [shares[0] * sum0[s]]
        for share, (level, _, _, total) in zip(shares[1:], rest):
            weighted.append(share * full(total, level, s))
        inv = 1.0 / (weighted[0] + weighted[1] + weighted[2] + weighted[3])
        merged = widened(shares[0] * inv) * acc0[s]
        for i, (level, acc, _, _) in enumerate(rest):
            factor = widened((weighted if level == 3 else shares)[i + 1] * inv)
            merged = merged + factor * full(acc, level, s).astype(F32)
        return jnp.dot(unperm[...], merged.astype(BF), preferred_element_type=F32).astype(BF)

    msend[...] = merge(1)
    m_copy.start()
    out_ref[:, mine] = merge(0)

    @pl.when(is_centre)
    def _():
        for c in l4_mirror + l3_mirror + [l4_fwd_mirror, l4_fwd_pair2, l4_fwd_pair3, l3_fwd, l3_out, l3_stat]:
            c.wait_send()

    @pl.when(is_end)
    def _():
        l3_q.wait_send()

    for c in [kv_copy, q_copy, l4_sib, l3_sib, l2_sib] + l4_pair + l2_pair + y_q + y_acc + y_stat:
        c.wait_send()
    m_copy.wait()


def project(merged_ref, w_ref, out_hbm, out_ref, sem):
    half = ROWS // 2
    stores = []
    for i in range(2):
        rows = pl.ds(i * half, half)
        out_ref[rows] = jnp.dot(merged_ref[rows], w_ref[...], preferred_element_type=F32).astype(BF)
        stores.append(pltpu.make_async_copy(out_ref.at[rows], out_hbm.at[rows], sem.at[i]))
        stores[i].start()
    for c in stores:
        c.wait()


def body(queries, keys, values, offsets, out_weight):
    n = [2 * k for k in KEPT]
    bf = [
        (ROWS, WIDTH), (ROWS, WIDTH), (ROWS, WIDTH), (3, ROWS, HALF), (2, 3, ROWS, HALF), (2, n[1], HALF),
        (2, 2, 2, KEPT[2], HALF), (4, 2, 2, KEPT[3], HALF), (4, 2, 2, KEPT[4], HALF),
        (2, KEPT[2], HALF), (2, KEPT[3], HALF), (2, KEPT[4], HALF),
        (n[1], HALF), (n[2], HALF), (2 * n[3], HALF), (4, n[4], HALF),
    ]
    scratch = [pltpu.VMEM((5, 16), jnp.int32)] + [pltpu.VMEM(shape, BF) for shape in bf]
    for width in (HALF, 128, 128):
        scratch += [pltpu.VMEM(shape, F32) for shape in [
            (2, ROWS, width), (n[1], width), (n[2], width), (2 * n[3], width), (4 * n[4], width)]]
    scratch += [
        pltpu.VMEM((n[3], HALF), BF), pltpu.VMEM((n[3], 128), F32), pltpu.VMEM((n[3], 128), F32),
        pltpu.VMEM((n[3], HALF), BF), pltpu.VMEM((n[3], HALF), BF),
        pltpu.VMEM((32, 128), F32), pltpu.VMEM((32, 128), F32),
        pltpu.VMEM((3 * n[4], HALF), BF), pltpu.VMEM((2, 32, 128), F32), pltpu.VMEM((3, n[4], HALF), BF), pltpu.VMEM((3, 32, 128), F32),
        pltpu.VMEM((n[4], HALF), F32), pltpu.VMEM((n[4], 128), F32), pltpu.VMEM((n[4], 128), F32),
        pltpu.VMEM((ROWS, ROWS), BF),
        pltpu.VMEM((ROWS, HALF), BF),
        pltpu.SemaphoreType.DMA((4,)),
        pltpu.SemaphoreType.DMA((36,)),
        pltpu.SemaphoreType.DMA((36,)),
    ]
    vmem = pl.BlockSpec(memory_space=pltpu.VMEM)
    anywhere = pl.BlockSpec(memory_space=pl.ANY)
    merged = pl.pallas_call(
        kernel,
        out_shape=pltpu.VMEM((ROWS, WIDTH), BF),
        in_specs=[anywhere] * 4,
        out_specs=vmem,
        scratch_shapes=scratch,
        compiler_params=pltpu.CompilerParams(collective_id=0, has_side_effects=True, vmem_limit_bytes=40 << 20),
        cost_estimate=pl.CostEstimate(flops=3 * 10**9, bytes_accessed=5 * 10**6, transcendentals=9 * 10**6),
        name="dilated_attention",
    )(*[pltpu.with_memory_space_constraint(x, pltpu.HBM) for x in (offsets, queries, keys, values)])
    return pl.pallas_call(
        project,
        out_shape=jax.ShapeDtypeStruct((ROWS, WIDTH), BF),
        in_specs=[vmem, vmem],
        out_specs=anywhere,
        scratch_shapes=[pltpu.VMEM((ROWS, WIDTH), BF), pltpu.SemaphoreType.DMA((2,))],
        compiler_params=pltpu.CompilerParams(vmem_limit_bytes=16 << 20),
        name="projection",
    )(merged, pltpu.with_memory_space_constraint(out_weight, pltpu.VMEM))


def solution(mesh):
    return jax.shard_map(
        body,
        mesh=mesh,
        in_specs=(P(("dp", "seq"), None), P(("dp", "seq"), None), P(("dp", "seq"), None), P(), P()),
        out_specs=P(("dp", "seq"), None),
        check_vma=False,
    )
```

```python
import math

import jax
import jax.numpy as jnp
from jax import lax
from jax.experimental import pallas as pl
from jax.experimental.pallas import tpu as pltpu
from jax.sharding import PartitionSpec as P

MESH = pl.DeviceIdType.MESH
BF = jnp.bfloat16
F32 = jnp.float32
ROWS = 512
WIDTH = 768
HALF = 384
HD = 48
NH = 8
COEF = math.log2(math.e) / math.sqrt(HD)
NT = (((1,), (1,)), ((), ()))
KEPT = [ROWS >> level for level in range(5)]


def reversed_bits(x, bits):
    out = jnp.zeros_like(x)
    for b in range(bits):
        out = out + ((x >> b) & 1) * (1 << (bits - 1 - b))
    return out


def window(first, count):
    lo, hi = HD * first, HD * (first + count)
    start = lo // 128 * 128
    width = 128 if hi <= start + 128 else 256
    return start, width


def head_mask(head, start, width):
    lane = lax.broadcasted_iota(jnp.int32, (1, width), 1) + start
    return (lane >= HD * head) & (lane < HD * head + HD)


def softmax_unit(s, v):
    top = jnp.max(s, axis=1, keepdims=True) * COEF
    p = jnp.exp2(s * COEF - top)
    total = jnp.sum(p, axis=1, keepdims=True)
    o = jnp.dot(p.astype(BF), v, preferred_element_type=F32)
    return o, top, total


def kernel(
    off_hbm, q_hbm, k_hbm, v_hbm, out_ref,
    off_ref, q_ref, k_ref, v_ref, stage, halves, s1, c2, c3, c4, x2, x3, x4, q1, q2, q3, qy,
    acc0, acc1, acc2, acc3, acc4, top0, top1, top2, top3, top4,
    sum0, sum1, sum2, sum3, sum4, o3, t3, u3, o3_out, o3_in, st3_out, st3_in, acc4_out, st4_out, acc4_in, st4_in, m4, t4, u4,
    unperm, msend, local_sem, send_sem, recv_sem,
):
    me = lax.axis_index("seq")
    core = lax.rem(me, 2)
    z = lax.rem(me // 2, 4)
    y = me // 8

    loads = [
        pltpu.make_async_copy(src, dst, local_sem.at[i])
        for i, (src, dst) in enumerate([(k_hbm, k_ref), (v_hbm, v_ref), (q_hbm, q_ref), (off_hbm, off_ref)])
    ]
    for i in (3, 0, 1, 2):
        loads[i].start()

    def at(yy, zz, cc):
        return {"seq": (yy * 4 + zz) * 2 + cc}

    z_pair = z + 1 - 2 * lax.rem(z, 2)
    sibling = at(y, z, 1 - core)
    pair, pair_other = at(y, z_pair, core), at(y, z_pair, 1 - core)
    mirror, mirror_other = at(y, 3 - z, core), at(y, 3 - z, 1 - core)
    y_next = [at(lax.rem(y + d, 4), z, core) for d in (1, 2, 3)]
    y_back = [at(lax.rem(y + 4 - d, 4), z, core) for d in (1, 2, 3)]
    is_centre = (z + 1) // 2 == 1
    is_end = jnp.logical_not(is_centre)
    barrier = pltpu.get_barrier_semaphore()
    for peer in [sibling, pair, pair_other, mirror, mirror_other] + y_next:
        pl.semaphore_signal(barrier, inc=1, device_id=peer, device_id_type=MESH)

    def remote(send, recv, src, dst, peer):
        return pltpu.make_async_remote_copy(
            src_ref=src, dst_ref=dst, send_sem=send_sem.at[send], recv_sem=recv_sem.at[recv],
            device_id=peer, device_id_type=MESH,
        )

    kv_copy = remote(0, 0, stage.at[pl.ds(0, 2)], halves.at[1, pl.ds(0, 2)], sibling)
    q_copy = remote(1, 1, stage.at[2], halves.at[1, 2], sibling)
    def spread_out(first, slots, extra):
        return [
            remote(first, first, extra, slots.at[0, core], sibling),
            remote(first + 1, first + 1, slots.at[0, core], slots.at[1, core], pair),
            remote(first + 2, first + 2, extra, slots.at[1, core], pair_other),
        ]

    def to_mirror(first, slots, extra):
        return [
            remote(first, first, slots.at[0, core], slots.at[2, core], mirror),
            remote(first + 1, first + 1, extra, slots.at[2, core], mirror_other),
        ]

    l4_sib, *l4_pair = spread_out(2, c4, x4)
    l3_sib, *l3_pair = spread_out(5, c3, x3)
    l2_sib = remote(8, 8, x2, c2.at[0, core], sibling)
    l2_pair = []
    for t in range(3):
        tile = pl.ds(128 * t, 128)
        l2_pair += [
            remote(9 + 2 * t, 9 + 2 * t, c2.at[0, core, :, :, tile], c2.at[1, core, :, :, tile], pair),
            remote(10 + 2 * t, 10 + 2 * t, x2.at[:, :, tile], c2.at[1, core, :, :, tile], pair_other),
        ]
    l4_mirror = to_mirror(15, c4, x4)
    l3_mirror = to_mirror(17, c3, x3)
    l4_fwd_mirror = remote(19, 19, c4.at[1], c4.at[3], mirror)
    l4_fwd_pair2 = remote(20, 19, c4.at[2], c4.at[3], pair)
    l3_fwd = remote(22, 21, c3.at[1], c3.at[3], mirror)
    n3 = 2 * KEPT[3]
    l3_q = remote(23, 22, q3.at[pl.ds(0, n3)], q3.at[pl.ds(n3, n3)], pair)
    l3_out = remote(24, 23, o3_out, o3_in, pair)
    l3_stat = remote(25, 24, st3_out, st3_in, pair)
    n4 = 2 * KEPT[4]
    y_q = [remote(26 + i, 26 + i, qy.at[0], qy.at[i + 1], y_next[i]) for i in range(3)]
    y_acc = [remote(29 + i, 29 + i, acc4_out.at[pl.ds(i * n4, n4)], acc4_in.at[i], y_back[i]) for i in range(3)]
    y_stat = [remote(32 + i, 32 + i, st4_out.at[(i + 1) // 2], st4_in.at[i], y_back[i]) for i in range(3)]
    m_copy = remote(35, 35, msend, out_ref.at[:, pl.ds(pl.multiple_of(core * HALF, 128), HALF)], sibling)

    dest = lax.broadcasted_iota(jnp.int32, (ROWS, 1), 0)
    source = (dest & 31) * 16 + reversed_bits(dest >> 5, 4)
    lane512 = lax.broadcasted_iota(jnp.int32, (ROWS, ROWS), 1)
    perm = jnp.where(lane512 == source, 1.0, 0.0).astype(BF)
    mine = pl.ds(pl.multiple_of(core * HALF, 128), HALF)
    theirs = pl.ds(pl.multiple_of((1 - core) * HALF, 128), HALF)

    def permuted(ref, lanes):
        return jnp.dot(perm, ref[:, lanes], preferred_element_type=F32).astype(BF)

    loads[3].wait()
    offs = off_ref[...].astype(BF)

    def reversed_offsets(heads):
        row = lax.broadcasted_iota(jnp.int32, heads.shape, 0)
        spread = jnp.dot(offs, jnp.where(row == heads, 1.0, 0.0).astype(BF), preferred_element_type=F32)
        return [None] + [reversed_bits(spread[level:level + 1].astype(jnp.int32), level) for level in range(1, 5)]

    column = lax.broadcasted_iota(jnp.int32, (16, HALF), 1) // HD
    mine_cols = reversed_offsets(column + NH * core)
    theirs_cols = reversed_offsets(column + NH * (1 - core))
    block_stat = reversed_offsets((lax.broadcasted_iota(jnp.int32, (16, 128), 1) & 7) + NH * core)

    def select(block, cols, level):
        n = KEPT[level]
        kept = block[0:n]
        for b in range(1, 1 << level):
            kept = jnp.where(cols[level] == b, block[b * n:(b + 1) * n], kept)
        return kept

    for kind, ref in enumerate([k_ref, v_ref]):
        loads[kind].wait()
        halves[0, kind] = permuted(ref, mine)
        stage[kind] = permuted(ref, theirs)
        c4[0, core, kind] = select(halves.at[0, kind], mine_cols, 4)
        x4[kind] = select(stage.at[kind], theirs_cols, 4)
    pl.semaphore_wait(barrier, 8)
    for c in l4_pair + l4_mirror:
        c.start()

    for kind in range(2):
        c3[0, core, kind] = select(halves.at[0, kind], mine_cols, 3)
        x3[kind] = select(stage.at[kind], theirs_cols, 3)

    @pl.when(is_centre)
    def _():
        for c in l3_mirror:
            c.start()

    @pl.when(is_end)
    def _():
        for c in l3_pair:
            c.start()

    l4_sib.start()
    l3_sib.start()
    kv_copy.start()
    loads[2].wait()
    stage[2] = permuted(q_ref, theirs)
    q_copy.start()
    for kind in range(2):
        c2[0, core, kind] = select(halves.at[0, kind], mine_cols, 2)
        x2[kind] = select(stage.at[kind], theirs_cols, 2)

    @pl.when(is_centre)
    def _():
        for c in l2_pair:
            c.start()

    l2_sib.start()
    halves[0, 2] = permuted(q_ref, mine)
    for src in range(2):
        if src == 1:
            q_copy.wait_recv()
        block = halves.at[src, 2]
        qy[0, src * KEPT[4]:(src + 1) * KEPT[4]] = select(block, mine_cols, 4)
        q3[src * KEPT[3]:(src + 1) * KEPT[3]] = select(block, mine_cols, 3)
    for c in y_q:
        c.start()

    @pl.when(is_end)
    def _():
        l3_q.start()

    stat_lane = lax.broadcasted_iota(jnp.int32, (1, 128), 1) & 7

    def attend(q_of, k_of, v_of, group, rows, acc, top_ref, sum_ref, heads=(0, NH), norm=False):
        tops = jnp.zeros((rows, 128), F32) if heads[0] == 0 else top_ref[...]
        sums = jnp.zeros((rows, 128), F32) if heads[0] == 0 else sum_ref[...]
        written = {t for t in range(0, HALF, 128) if t < HD * heads[0]}

        def scores(first):
            start, width = window(first, group)
            masks = [head_mask(first + g, start, width) for g in range(group)]
            q, k = q_of(start, width), k_of(start, width)
            if group == 1:
                k = jnp.where(masks[0], k, jnp.zeros((), BF))
            else:
                q = jnp.concatenate([jnp.where(m, q, jnp.zeros((), BF)) for m in masks], axis=0)
            return lax.dot_general(q, k, NT, preferred_element_type=F32)

        following = scores(heads[0])
        for first in range(heads[0], heads[1], group):
            start, width = window(first, group)
            masks = [head_mask(first + g, start, width) for g in range(group)]
            s = following
            if first + group < heads[1]:
                following = scores(first + group)
            o, top, total = softmax_unit(s, v_of(start, width))
            if norm:
                o = o * (1.0 / total)
            for t in range(start, start + width, 128):
                part = None
                for g in range(group):
                    lo, hi = HD * (first + g), HD * (first + g + 1)
                    if hi <= t or lo >= t + 128:
                        continue
                    piece = o[g * rows:(g + 1) * rows, t - start:t - start + 128]
                    mask = masks[g][:, t - start:t - start + 128]
                    if part is None:
                        part = jnp.where(mask, piece, acc[:, t:t + 128]) if t in written else piece
                    else:
                        part = jnp.where(mask, piece, part)
                acc[:, t:t + 128] = part
                written.add(t)
            for g in range(group):
                lanes = stat_lane == first + g
                tops = jnp.where(lanes, top[g * rows:(g + 1) * rows], tops)
                sums = jnp.where(lanes, total[g * rows:(g + 1) * rows], sums)
        top_ref[...] = tops
        sum_ref[...] = sums

    def level0(s, heads):
        attend(
            lambda a, w: halves[s, 2, :, a:a + w],
            lambda a, w: halves[s, 0, :, a:a + w],
            lambda a, w: halves[s, 1, :, a:a + w],
            1, ROWS, acc0.at[s], top0.at[s], sum0.at[s], heads,
        )

    level0(0, (0, 4))

    @pl.when(is_centre)
    def _():
        for c in l4_pair:
            c.wait_recv()
        l4_fwd_mirror.start()
        for c in l4_mirror:
            c.wait_recv()
        l4_fwd_pair2.start()

    level0(0, (4, NH))

    kv_copy.wait_recv()
    level0(1, (0, 4))

    @pl.when(is_centre)
    def _():
        for c in l3_pair:
            c.wait_recv()
        l3_fwd.start()

    @pl.when(is_end)
    def _():
        for c in l3_pair:
            c.wait_send()
        for c in l2_pair:
            c.start()

    level0(1, (4, NH))
    for src in range(2):
        q2[src * KEPT[2]:(src + 1) * KEPT[2]] = select(halves.at[src, 2], mine_cols, 2)
        q1[src * KEPT[1]:(src + 1) * KEPT[1]] = select(halves.at[src, 2], mine_cols, 1)
        for kind in range(2):
            s1[kind, src * KEPT[1]:(src + 1) * KEPT[1]] = select(halves.at[src, kind], mine_cols, 1)

    def level1(heads):
        attend(
            lambda a, w: q1[:, a:a + w], lambda a, w: s1[0, :, a:a + w], lambda a, w: s1[1, :, a:a + w],
            1, 2 * KEPT[1], acc1, top1, sum1, heads,
        )

    level1((0, 4))

    @pl.when(is_centre)
    def _():
        l4_fwd_mirror.wait_recv()

    @pl.when(is_end)
    def _():
        for c in l4_pair:
            c.wait_recv()
        for c in l4_mirror:
            c.wait_recv()
        l4_fwd_pair2.wait_recv()

    l4_sib.wait_recv()
    for c in y_q:
        c.wait_recv()

    def chips(ref, kind, slots):
        return lambda a, w: jnp.concatenate(
            [ref[slot, tok, kind, :, a:a + w] for slot in range(slots) for tok in range(2)], axis=0)

    attend(
        lambda a, w: jnp.concatenate([qy[b, :, a:a + w] for b in range(4)], axis=0),
        chips(c4, 0, 4), chips(c4, 1, 4), 2, 4 * n4, acc4, top4, sum4, norm=True,
    )
    stat_all = lax.broadcasted_iota(jnp.int32, (1, 128), 1)
    acc4_out[...] = acc4[n4:].astype(BF)
    packed4 = jnp.where(stat_all < 16, top4[...], sum4[...])
    for i in range(2):
        st4_out[i] = packed4[128 * i:128 * (i + 1)].T[0:32]
    for c in y_acc + y_stat:
        c.start()
    l3_sib.wait_recv()

    def level3(start):
        rows = pl.ds(start, n3)
        attend(
            lambda a, w: q3[rows, a:a + w], chips(c3, 0, 4), chips(c3, 1, 4),
            4, n3, acc3.at[rows], top3.at[rows], sum3.at[rows], norm=True,
        )

    @pl.when(is_centre)
    def _():
        for c in l3_mirror:
            c.wait_recv()
        l3_fwd.wait_recv()
        l3_q.wait_recv()
        level3(n3)
        o3_out[...] = acc3[n3:].astype(BF)
        st3_out[...] = jnp.where(stat_all < 16, top3[n3:], sum3[n3:]).T[0:32]
        l3_out.start()
        l3_stat.start()

    level1((4, NH))
    back = reversed_bits(dest & 15, 4) * 32 + (dest >> 4)
    unperm[...] = jnp.where(lane512 == back, 1.0, 0.0).astype(BF)

    @pl.when(is_centre)
    def _():
        level3(0)
        o3[...] = acc3[0:n3].astype(BF)
        t3[...] = top3[0:n3]
        u3[...] = sum3[0:n3]

    row_class = lax.broadcasted_iota(jnp.int32, (ROWS, 1), 0) >> 5

    def full(ref, level, s):
        n = KEPT[level]
        return jnp.concatenate([ref[s * n:(s + 1) * n]] * (1 << level), axis=0)

    def full_top(ref, level, s):
        match = (row_class >> (4 - level)) == block_stat[level]
        return jnp.where(match, full(ref, level, s), -1e30)

    spread_row = lax.broadcasted_iota(jnp.int32, (128, HALF), 0)
    spread_col = lax.broadcasted_iota(jnp.int32, (128, HALF), 1) // HD
    spread = jnp.where((spread_row < 16) & ((spread_row & 7) == spread_col), 1.0, 0.0).astype(BF)

    def widened(weight):
        high = weight.astype(BF).astype(F32)
        low = jnp.where(stat_all < 16, weight - high, 0.0)
        packed = jnp.where(stat_all < 8, high, low).astype(BF)
        return jnp.dot(packed, spread, preferred_element_type=F32)

    for src in range(2):
        other = full_top(top1, 1, src)
        peak = jnp.maximum(top0[src], other)
        share0, share1 = jnp.exp2(top0[src] - peak), jnp.exp2(other - peak)
        top0[src] = peak
        sum0[src] = share0 * sum0[src] + share1 * full(sum1, 1, src)
        acc0[src] = widened(share0) * acc0[src] + widened(share1) * full(acc1, 1, src)

    l2_sib.wait_recv()
    for tile in range(3):
        for c in l2_pair[2 * tile:2 * tile + 2]:
            c.wait_recv()
        attend(
            lambda a, w: q2[:, a:a + w], chips(c2, 0, 2), chips(c2, 1, 2), 2, 2 * KEPT[2], acc2, top2, sum2,
            ((0, 2), (2, 4), (4, NH))[tile],
        )

    for c in y_acc + y_stat:
        c.wait_recv()
    zeros = jnp.zeros((112, 128), F32)

    def unpacked(stat):
        return [jnp.concatenate([stat[16 * i:16 * (i + 1)], zeros], axis=0).T for i in range(2)]

    tops4, sums4, accs4 = [top4[0:n4]], [sum4[0:n4]], [acc4[0:n4]]
    for i in range(3):
        at4 = (i + 1) % 2 * n4
        for part, stats in zip(unpacked(st4_in.at[i]), (tops4, sums4)):
            stats.append(part[at4:at4 + n4])
        accs4.append(acc4_in[i].astype(F32))
    peak4 = jnp.maximum(jnp.maximum(tops4[0], tops4[1]), jnp.maximum(tops4[2], tops4[3]))
    parts4 = [jnp.exp2(t - peak4) * total for t, total in zip(tops4, sums4)]
    t4[...] = peak4
    u4[...] = parts4[0] + parts4[1] + parts4[2] + parts4[3]
    total4 = widened(parts4[0]) * accs4[0]
    for i in range(1, 4):
        total4 = total4 + widened(parts4[i]) * accs4[i]
    m4[...] = total4

    @pl.when(is_end)
    def _():
        l3_out.wait_recv()
        l3_stat.wait_recv()
        o3[...] = o3_in[...]
        t3[...], u3[...] = unpacked(st3_in)

    rest = [(2, acc2, top2, sum2), (3, o3, t3, u3), (4, m4, t4, u4)]

    def merge(s):
        level_tops = [top0[s]] + [full_top(top, level, s) for level, _, top, _ in rest]
        peak = jnp.maximum(jnp.maximum(level_tops[0], level_tops[1]), jnp.maximum(level_tops[2], level_tops[3]))
        shares = [jnp.exp2(t - peak) for t in level_tops]
        weighted = [shares[0] * sum0[s]]
        for share, (level, _, _, total) in zip(shares[1:], rest):
            weighted.append(share * full(total, level, s))
        inv = 1.0 / (weighted[0] + weighted[1] + weighted[2] + weighted[3])
        merged = widened(shares[0] * inv) * acc0[s]
        for i, (level, acc, _, _) in enumerate(rest):
            factor = widened((weighted if level == 3 else shares)[i + 1] * inv)
            merged = merged + factor * full(acc, level, s).astype(F32)
        return jnp.dot(unperm[...], merged.astype(BF), preferred_element_type=F32).astype(BF)

    msend[...] = merge(1)
    m_copy.start()
    out_ref[:, mine] = merge(0)

    @pl.when(is_centre)
    def _():
        for c in l3_mirror + [l4_fwd_mirror, l4_fwd_pair2, l3_fwd, l3_out, l3_stat]:
            c.wait_send()

    @pl.when(is_end)
    def _():
        l3_q.wait_send()

    for c in [kv_copy, q_copy, l4_sib, l3_sib, l2_sib] + l4_pair + l4_mirror + l2_pair + y_q + y_acc + y_stat:
        c.wait_send()
    m_copy.wait()


def project(merged_ref, w_ref, out_hbm, out_ref, sem):
    half = ROWS // 2
    stores = []
    for i in range(2):
        rows = pl.ds(i * half, half)
        out_ref[rows] = jnp.dot(merged_ref[rows], w_ref[...], preferred_element_type=F32).astype(BF)
        stores.append(pltpu.make_async_copy(out_ref.at[rows], out_hbm.at[rows], sem.at[i]))
        stores[i].start()
    for c in stores:
        c.wait()


def body(queries, keys, values, offsets, out_weight):
    n = [2 * k for k in KEPT]
    bf = [
        (ROWS, WIDTH), (ROWS, WIDTH), (ROWS, WIDTH), (3, ROWS, HALF), (2, 3, ROWS, HALF), (2, n[1], HALF),
        (2, 2, 2, KEPT[2], HALF), (4, 2, 2, KEPT[3], HALF), (4, 2, 2, KEPT[4], HALF),
        (2, KEPT[2], HALF), (2, KEPT[3], HALF), (2, KEPT[4], HALF),
        (n[1], HALF), (n[2], HALF), (2 * n[3], HALF), (4, n[4], HALF),
    ]
    scratch = [pltpu.VMEM((5, 16), jnp.int32)] + [pltpu.VMEM(shape, BF) for shape in bf]
    for width in (HALF, 128, 128):
        scratch += [pltpu.VMEM(shape, F32) for shape in [
            (2, ROWS, width), (n[1], width), (n[2], width), (2 * n[3], width), (4 * n[4], width)]]
    scratch += [
        pltpu.VMEM((n[3], HALF), BF), pltpu.VMEM((n[3], 128), F32), pltpu.VMEM((n[3], 128), F32),
        pltpu.VMEM((n[3], HALF), BF), pltpu.VMEM((n[3], HALF), BF),
        pltpu.VMEM((32, 128), F32), pltpu.VMEM((32, 128), F32),
        pltpu.VMEM((3 * n[4], HALF), BF), pltpu.VMEM((2, 32, 128), F32), pltpu.VMEM((3, n[4], HALF), BF), pltpu.VMEM((3, 32, 128), F32),
        pltpu.VMEM((n[4], HALF), F32), pltpu.VMEM((n[4], 128), F32), pltpu.VMEM((n[4], 128), F32),
        pltpu.VMEM((ROWS, ROWS), BF),
        pltpu.VMEM((ROWS, HALF), BF),
        pltpu.SemaphoreType.DMA((4,)),
        pltpu.SemaphoreType.DMA((36,)),
        pltpu.SemaphoreType.DMA((36,)),
    ]
    vmem = pl.BlockSpec(memory_space=pltpu.VMEM)
    anywhere = pl.BlockSpec(memory_space=pl.ANY)
    merged = pl.pallas_call(
        kernel,
        out_shape=pltpu.VMEM((ROWS, WIDTH), BF),
        in_specs=[anywhere] * 4,
        out_specs=vmem,
        scratch_shapes=scratch,
        compiler_params=pltpu.CompilerParams(collective_id=0, has_side_effects=True, vmem_limit_bytes=40 << 20),
        cost_estimate=pl.CostEstimate(flops=3 * 10**9, bytes_accessed=5 * 10**6, transcendentals=9 * 10**6),
        name="dilated_attention",
    )(*[pltpu.with_memory_space_constraint(x, pltpu.HBM) for x in (offsets, queries, keys, values)])
    return pl.pallas_call(
        project,
        out_shape=jax.ShapeDtypeStruct((ROWS, WIDTH), BF),
        in_specs=[vmem, vmem],
        out_specs=anywhere,
        scratch_shapes=[pltpu.VMEM((ROWS, WIDTH), BF), pltpu.SemaphoreType.DMA((2,))],
        compiler_params=pltpu.CompilerParams(vmem_limit_bytes=16 << 20),
        name="projection",
    )(merged, pltpu.with_memory_space_constraint(out_weight, pltpu.VMEM))


def solution(mesh):
    return jax.shard_map(
        body,
        mesh=mesh,
        in_specs=(P(("dp", "seq"), None), P(("dp", "seq"), None), P(("dp", "seq"), None), P(), P()),
        out_specs=P(("dp", "seq"), None),
        check_vma=False,
    )
```

```python
import math

import jax
import jax.numpy as jnp
from jax import lax
from jax.experimental import pallas as pl
from jax.experimental.pallas import tpu as pltpu
from jax.sharding import PartitionSpec as P

MESH = pl.DeviceIdType.MESH
BF = jnp.bfloat16
F32 = jnp.float32
ROWS = 512
WIDTH = 768
HALF = 384
HD = 48
NH = 8
COEF = math.log2(math.e) / math.sqrt(HD)
NT = (((1,), (1,)), ((), ()))
KEPT = [ROWS >> level for level in range(5)]


def reversed_bits(x, bits):
    out = jnp.zeros_like(x)
    for b in range(bits):
        out = out + ((x >> b) & 1) * (1 << (bits - 1 - b))
    return out


def window(first, count):
    lo, hi = HD * first, HD * (first + count)
    start = lo // 128 * 128
    width = 128 if hi <= start + 128 else 256
    return start, width


def head_mask(head, start, width):
    lane = lax.broadcasted_iota(jnp.int32, (1, width), 1) + start
    return (lane >= HD * head) & (lane < HD * head + HD)


def softmax_unit(s, v):
    top = jnp.max(s, axis=1, keepdims=True) * COEF
    p = jnp.exp2(s * COEF - top)
    total = jnp.sum(p, axis=1, keepdims=True)
    o = jnp.dot(p.astype(BF), v, preferred_element_type=F32)
    return o, top, total


def kernel(
    off_hbm, q_hbm, k_hbm, v_hbm, out_ref,
    off_ref, q_ref, k_ref, v_ref, stage, halves, s1, c2, c3, c4, x2, x3, x4, q1, q2, q3, qy,
    acc0, acc1, acc2, acc3, acc4, top0, top1, top2, top3, top4,
    sum0, sum1, sum2, sum3, sum4, o3, t3, u3, o3_out, o3_in, st3_out, st3_in, acc4_out, st4_out, acc4_in, st4_in, m4, t4, u4,
    unperm, msend, local_sem, send_sem, recv_sem,
):
    me = lax.axis_index("seq")
    core = lax.rem(me, 2)
    z = lax.rem(me // 2, 4)
    y = me // 8

    loads = [
        pltpu.make_async_copy(src, dst, local_sem.at[i])
        for i, (src, dst) in enumerate([(k_hbm, k_ref), (v_hbm, v_ref), (q_hbm, q_ref), (off_hbm, off_ref)])
    ]
    for i in (3, 0, 1, 2):
        loads[i].start()

    def at(yy, zz, cc):
        return {"seq": (yy * 4 + zz) * 2 + cc}

    z_pair = z + 1 - 2 * lax.rem(z, 2)
    sibling = at(y, z, 1 - core)
    pair, pair_other = at(y, z_pair, core), at(y, z_pair, 1 - core)
    mirror, mirror_other = at(y, 3 - z, core), at(y, 3 - z, 1 - core)
    y_next = [at(lax.rem(y + d, 4), z, core) for d in (1, 2, 3)]
    y_back = [at(lax.rem(y + 4 - d, 4), z, core) for d in (1, 2, 3)]
    is_centre = (z + 1) // 2 == 1
    is_end = jnp.logical_not(is_centre)
    barrier = pltpu.get_barrier_semaphore()
    for peer in [sibling, pair, pair_other, mirror, mirror_other] + y_next:
        pl.semaphore_signal(barrier, inc=1, device_id=peer, device_id_type=MESH)

    def remote(send, recv, src, dst, peer):
        return pltpu.make_async_remote_copy(
            src_ref=src, dst_ref=dst, send_sem=send_sem.at[send], recv_sem=recv_sem.at[recv],
            device_id=peer, device_id_type=MESH,
        )

    kv_copy = remote(0, 0, stage.at[pl.ds(0, 2)], halves.at[1, pl.ds(0, 2)], sibling)
    q_copy = remote(1, 1, stage.at[2], halves.at[1, 2], sibling)
    def spread_out(first, slots, extra):
        return [
            remote(first, first, extra, slots.at[0, core], sibling),
            remote(first + 1, first + 1, slots.at[0, core], slots.at[1, core], pair),
            remote(first + 2, first + 2, extra, slots.at[1, core], pair_other),
        ]

    def to_mirror(first, slots, extra):
        return [
            remote(first, first, slots.at[0, core], slots.at[2, core], mirror),
            remote(first + 1, first + 1, extra, slots.at[2, core], mirror_other),
        ]

    l4_sib, *l4_pair = spread_out(2, c4, x4)
    l3_sib, *l3_pair = spread_out(5, c3, x3)
    l2_sib = remote(8, 8, x2, c2.at[0, core], sibling)
    l2_pair = []
    for t in range(3):
        l2_pair += [
            remote(9 + 2 * t, 9 + 2 * t, c2.at[0, core, t], c2.at[1, core, t], pair),
            remote(10 + 2 * t, 10 + 2 * t, x2.at[t], c2.at[1, core, t], pair_other),
        ]
    l4_mirror = to_mirror(15, c4, x4)
    l3_mirror = to_mirror(17, c3, x3)
    l4_fwd_mirror = remote(19, 19, c4.at[1], c4.at[3], mirror)
    l4_fwd_pair2 = remote(20, 19, c4.at[2], c4.at[3], pair)
    l3_fwd = remote(22, 21, c3.at[1], c3.at[3], mirror)
    n3 = 2 * KEPT[3]
    l3_q = remote(23, 22, q3.at[pl.ds(0, n3)], q3.at[pl.ds(n3, n3)], pair)
    l3_out = remote(24, 23, o3_out, o3_in, pair)
    l3_stat = remote(25, 24, st3_out, st3_in, pair)
    n4 = 2 * KEPT[4]
    y_q = [remote(26 + i, 26 + i, qy.at[0], qy.at[i + 1], y_next[i]) for i in range(3)]
    y_acc = [remote(29 + i, 29 + i, acc4_out.at[pl.ds(i * n4, n4)], acc4_in.at[i], y_back[i]) for i in range(3)]
    y_stat = [remote(32 + i, 32 + i, st4_out.at[(i + 1) // 2], st4_in.at[i], y_back[i]) for i in range(3)]
    m_copy = remote(35, 35, msend, out_ref.at[:, pl.ds(pl.multiple_of(core * HALF, 128), HALF)], sibling)

    dest = lax.broadcasted_iota(jnp.int32, (ROWS, 1), 0)
    source = (dest & 31) * 16 + reversed_bits(dest >> 5, 4)
    lane512 = lax.broadcasted_iota(jnp.int32, (ROWS, ROWS), 1)
    perm = jnp.where(lane512 == source, 1.0, 0.0).astype(BF)
    mine = pl.ds(pl.multiple_of(core * HALF, 128), HALF)
    theirs = pl.ds(pl.multiple_of((1 - core) * HALF, 128), HALF)

    def permuted(ref, lanes):
        return jnp.dot(perm, ref[:, lanes], preferred_element_type=F32).astype(BF)

    loads[3].wait()
    offs = off_ref[...].astype(BF)

    def reversed_offsets(heads):
        row = lax.broadcasted_iota(jnp.int32, heads.shape, 0)
        spread = jnp.dot(offs, jnp.where(row == heads, 1.0, 0.0).astype(BF), preferred_element_type=F32)
        return [None] + [reversed_bits(spread[level:level + 1].astype(jnp.int32), level) for level in range(1, 5)]

    column = lax.broadcasted_iota(jnp.int32, (16, HALF), 1) // HD
    mine_cols = reversed_offsets(column + NH * core)
    theirs_cols = reversed_offsets(column + NH * (1 - core))
    block_stat = reversed_offsets((lax.broadcasted_iota(jnp.int32, (16, 128), 1) & 7) + NH * core)

    def select(block, cols, level):
        n = KEPT[level]
        kept = block[0:n]
        for b in range(1, 1 << level):
            kept = jnp.where(cols[level] == b, block[b * n:(b + 1) * n], kept)
        return kept

    for kind, ref in enumerate([k_ref, v_ref]):
        loads[kind].wait()
        halves[0, kind] = permuted(ref, mine)
        stage[kind] = permuted(ref, theirs)
        c4[0, core, kind] = select(halves.at[0, kind], mine_cols, 4)
        x4[kind] = select(stage.at[kind], theirs_cols, 4)
    pl.semaphore_wait(barrier, 8)
    for c in l4_pair + l4_mirror:
        c.start()

    for kind in range(2):
        c3[0, core, kind] = select(halves.at[0, kind], mine_cols, 3)
        x3[kind] = select(stage.at[kind], theirs_cols, 3)

    @pl.when(is_centre)
    def _():
        for c in l3_mirror:
            c.start()

    @pl.when(is_end)
    def _():
        for c in l3_pair:
            c.start()

    l4_sib.start()
    l3_sib.start()
    kv_copy.start()
    loads[2].wait()
    stage[2] = permuted(q_ref, theirs)
    q_copy.start()
    for kind in range(2):
        own_rows = select(halves.at[0, kind], mine_cols, 2)
        other_rows = select(stage.at[kind], theirs_cols, 2)
        for t in range(3):
            c2[0, core, t, kind] = own_rows[:, 128 * t:128 * t + 128]
            x2[t, kind] = other_rows[:, 128 * t:128 * t + 128]

    @pl.when(is_centre)
    def _():
        for c in l2_pair:
            c.start()

    l2_sib.start()
    halves[0, 2] = permuted(q_ref, mine)
    for src in range(2):
        if src == 1:
            q_copy.wait_recv()
        block = halves.at[src, 2]
        qy[0, src * KEPT[4]:(src + 1) * KEPT[4]] = select(block, mine_cols, 4)
        q3[src * KEPT[3]:(src + 1) * KEPT[3]] = select(block, mine_cols, 3)
    for c in y_q:
        c.start()

    @pl.when(is_end)
    def _():
        l3_q.start()

    stat_lane = lax.broadcasted_iota(jnp.int32, (1, 128), 1) & 7

    def attend(q_of, k_of, v_of, group, rows, acc, top_ref, sum_ref, heads=(0, NH), norm=False):
        tops = jnp.zeros((rows, 128), F32) if heads[0] == 0 else top_ref[...]
        sums = jnp.zeros((rows, 128), F32) if heads[0] == 0 else sum_ref[...]
        written = {t for t in range(0, HALF, 128) if t < HD * heads[0]}

        def scores(first):
            start, width = window(first, group)
            masks = [head_mask(first + g, start, width) for g in range(group)]
            q, k = q_of(start, width), k_of(start, width)
            if group == 1:
                k = jnp.where(masks[0], k, jnp.zeros((), BF))
            else:
                q = jnp.concatenate([jnp.where(m, q, jnp.zeros((), BF)) for m in masks], axis=0)
            return lax.dot_general(q, k, NT, preferred_element_type=F32)

        following = None
        for first in range(heads[0], heads[1], group):
            start, width = window(first, group)
            masks = [head_mask(first + g, start, width) for g in range(group)]
            s = following if following is not None else scores(first)
            following = scores(first + 1) if group == 1 and first + 1 < heads[1] else None
            o, top, total = softmax_unit(s, v_of(start, width))
            if norm:
                o = o * (1.0 / total)
            for t in range(start, start + width, 128):
                part = None
                for g in range(group):
                    lo, hi = HD * (first + g), HD * (first + g + 1)
                    if hi <= t or lo >= t + 128:
                        continue
                    piece = o[g * rows:(g + 1) * rows, t - start:t - start + 128]
                    mask = masks[g][:, t - start:t - start + 128]
                    if part is None:
                        part = jnp.where(mask, piece, acc[:, t:t + 128]) if t in written else piece
                    else:
                        part = jnp.where(mask, piece, part)
                acc[:, t:t + 128] = part
                written.add(t)
            for g in range(group):
                lanes = stat_lane == first + g
                tops = jnp.where(lanes, top[g * rows:(g + 1) * rows], tops)
                sums = jnp.where(lanes, total[g * rows:(g + 1) * rows], sums)
        top_ref[...] = tops
        sum_ref[...] = sums

    def level0(s, heads):
        attend(
            lambda a, w: halves[s, 2, :, a:a + w],
            lambda a, w: halves[s, 0, :, a:a + w],
            lambda a, w: halves[s, 1, :, a:a + w],
            1, ROWS, acc0.at[s], top0.at[s], sum0.at[s], heads,
        )

    level0(0, (0, 4))

    @pl.when(is_centre)
    def _():
        for c in l4_pair:
            c.wait_recv()
        l4_fwd_mirror.start()
        for c in l4_mirror:
            c.wait_recv()
        l4_fwd_pair2.start()

    level0(0, (4, NH))

    kv_copy.wait_recv()
    level0(1, (0, 4))

    @pl.when(is_centre)
    def _():
        for c in l3_pair:
            c.wait_recv()
        l3_fwd.start()

    @pl.when(is_end)
    def _():
        for c in l3_pair:
            c.wait_send()
        for c in l2_pair:
            c.start()

    level0(1, (4, NH))
    for src in range(2):
        q2[src * KEPT[2]:(src + 1) * KEPT[2]] = select(halves.at[src, 2], mine_cols, 2)
        q1[src * KEPT[1]:(src + 1) * KEPT[1]] = select(halves.at[src, 2], mine_cols, 1)
        for kind in range(2):
            s1[kind, src * KEPT[1]:(src + 1) * KEPT[1]] = select(halves.at[src, kind], mine_cols, 1)

    def level1(heads):
        attend(
            lambda a, w: q1[:, a:a + w], lambda a, w: s1[0, :, a:a + w], lambda a, w: s1[1, :, a:a + w],
            1, 2 * KEPT[1], acc1, top1, sum1, heads,
        )

    level1((0, 4))

    @pl.when(is_centre)
    def _():
        l4_fwd_mirror.wait_recv()

    @pl.when(is_end)
    def _():
        for c in l4_pair:
            c.wait_recv()
        for c in l4_mirror:
            c.wait_recv()
        l4_fwd_pair2.wait_recv()

    l4_sib.wait_recv()
    for c in y_q:
        c.wait_recv()

    def chips(ref, kind, slots):
        return lambda a, w: jnp.concatenate(
            [ref[slot, tok, kind, :, a:a + w] for slot in range(slots) for tok in range(2)], axis=0)

    attend(
        lambda a, w: jnp.concatenate([qy[b, :, a:a + w] for b in range(4)], axis=0),
        chips(c4, 0, 4), chips(c4, 1, 4), 2, 4 * n4, acc4, top4, sum4, norm=True,
    )
    stat_all = lax.broadcasted_iota(jnp.int32, (1, 128), 1)
    acc4_out[...] = acc4[n4:].astype(BF)
    packed4 = jnp.where(stat_all < 16, top4[...], sum4[...])
    for i in range(2):
        st4_out[i] = packed4[128 * i:128 * (i + 1)].T[0:32]
    for c in y_acc + y_stat:
        c.start()
    l3_sib.wait_recv()

    def level3(start):
        rows = pl.ds(start, n3)
        attend(
            lambda a, w: q3[rows, a:a + w], chips(c3, 0, 4), chips(c3, 1, 4),
            4, n3, acc3.at[rows], top3.at[rows], sum3.at[rows], norm=True,
        )

    @pl.when(is_centre)
    def _():
        for c in l3_mirror:
            c.wait_recv()
        l3_fwd.wait_recv()
        l3_q.wait_recv()
        level3(n3)
        o3_out[...] = acc3[n3:].astype(BF)
        st3_out[...] = jnp.where(stat_all < 16, top3[n3:], sum3[n3:]).T[0:32]
        l3_out.start()
        l3_stat.start()

    level1((4, NH))
    back = reversed_bits(dest & 15, 4) * 32 + (dest >> 4)
    unperm[...] = jnp.where(lane512 == back, 1.0, 0.0).astype(BF)

    @pl.when(is_centre)
    def _():
        level3(0)
        o3[...] = acc3[0:n3].astype(BF)
        t3[...] = top3[0:n3]
        u3[...] = sum3[0:n3]

    row_class = lax.broadcasted_iota(jnp.int32, (ROWS, 1), 0) >> 5

    def full(ref, level, s):
        n = KEPT[level]
        return jnp.concatenate([ref[s * n:(s + 1) * n]] * (1 << level), axis=0)

    def full_top(ref, level, s):
        match = (row_class >> (4 - level)) == block_stat[level]
        return jnp.where(match, full(ref, level, s), -1e30)

    spread_row = lax.broadcasted_iota(jnp.int32, (128, HALF), 0)
    spread_col = lax.broadcasted_iota(jnp.int32, (128, HALF), 1) // HD
    spread = jnp.where((spread_row < 16) & ((spread_row & 7) == spread_col), 1.0, 0.0).astype(BF)

    def widened(weight):
        high = weight.astype(BF).astype(F32)
        low = jnp.where(stat_all < 16, weight - high, 0.0)
        packed = jnp.where(stat_all < 8, high, low).astype(BF)
        return jnp.dot(packed, spread, preferred_element_type=F32)

    for src in range(2):
        other = full_top(top1, 1, src)
        peak = jnp.maximum(top0[src], other)
        share0, share1 = jnp.exp2(top0[src] - peak), jnp.exp2(other - peak)
        top0[src] = peak
        sum0[src] = share0 * sum0[src] + share1 * full(sum1, 1, src)
        acc0[src] = widened(share0) * acc0[src] + widened(share1) * full(acc1, 1, src)

    l2_sib.wait_recv()
    def tiles2(kind):
        return lambda a, w: jnp.concatenate([
            jnp.concatenate([c2[slot, tok, t, kind] for t in range(a // 128, (a + w) // 128)], axis=1)
            for slot in range(2) for tok in range(2)], axis=0)

    for tile in range(3):
        for c in l2_pair[2 * tile:2 * tile + 2]:
            c.wait_recv()
        attend(
            lambda a, w: q2[:, a:a + w], tiles2(0), tiles2(1), 2, 2 * KEPT[2], acc2, top2, sum2,
            ((0, 2), (2, 4), (4, NH))[tile],
        )

    for c in y_acc + y_stat:
        c.wait_recv()
    zeros = jnp.zeros((112, 128), F32)

    def unpacked(stat):
        return [jnp.concatenate([stat[16 * i:16 * (i + 1)], zeros], axis=0).T for i in range(2)]

    tops4, sums4, accs4 = [top4[0:n4]], [sum4[0:n4]], [acc4[0:n4]]
    for i in range(3):
        at4 = (i + 1) % 2 * n4
        for part, stats in zip(unpacked(st4_in.at[i]), (tops4, sums4)):
            stats.append(part[at4:at4 + n4])
        accs4.append(acc4_in[i].astype(F32))
    peak4 = jnp.maximum(jnp.maximum(tops4[0], tops4[1]), jnp.maximum(tops4[2], tops4[3]))
    parts4 = [jnp.exp2(t - peak4) * total for t, total in zip(tops4, sums4)]
    t4[...] = peak4
    u4[...] = parts4[0] + parts4[1] + parts4[2] + parts4[3]
    total4 = widened(parts4[0]) * accs4[0]
    for i in range(1, 4):
        total4 = total4 + widened(parts4[i]) * accs4[i]
    m4[...] = total4

    @pl.when(is_end)
    def _():
        l3_out.wait_recv()
        l3_stat.wait_recv()
        o3[...] = o3_in[...]
        t3[...], u3[...] = unpacked(st3_in)

    rest = [(2, acc2, top2, sum2), (3, o3, t3, u3), (4, m4, t4, u4)]

    def merge(s):
        level_tops = [top0[s]] + [full_top(top, level, s) for level, _, top, _ in rest]
        peak = jnp.maximum(jnp.maximum(level_tops[0], level_tops[1]), jnp.maximum(level_tops[2], level_tops[3]))
        shares = [jnp.exp2(t - peak) for t in level_tops]
        weighted = [shares[0] * sum0[s]]
        for share, (level, _, _, total) in zip(shares[1:], rest):
            weighted.append(share * full(total, level, s))
        inv = 1.0 / (weighted[0] + weighted[1] + weighted[2] + weighted[3])
        merged = widened(shares[0] * inv) * acc0[s]
        for i, (level, acc, _, _) in enumerate(rest):
            factor = widened((weighted if level == 3 else shares)[i + 1] * inv)
            merged = merged + factor * full(acc, level, s).astype(F32)
        return jnp.dot(unperm[...], merged.astype(BF), preferred_element_type=F32).astype(BF)

    msend[...] = merge(1)
    m_copy.start()
    out_ref[:, mine] = merge(0)

    @pl.when(is_centre)
    def _():
        for c in l3_mirror + [l4_fwd_mirror, l4_fwd_pair2, l3_fwd, l3_out, l3_stat]:
            c.wait_send()

    @pl.when(is_end)
    def _():
        l3_q.wait_send()

    for c in [kv_copy, q_copy, l4_sib, l3_sib, l2_sib] + l4_pair + l4_mirror + l2_pair + y_q + y_acc + y_stat:
        c.wait_send()
    m_copy.wait()


def project(merged_ref, w_ref, out_hbm, out_ref, sem):
    half = ROWS // 2
    stores = []
    for i in range(2):
        rows = pl.ds(i * half, half)
        out_ref[rows] = jnp.dot(merged_ref[rows], w_ref[...], preferred_element_type=F32).astype(BF)
        stores.append(pltpu.make_async_copy(out_ref.at[rows], out_hbm.at[rows], sem.at[i]))
        stores[i].start()
    for c in stores:
        c.wait()


def body(queries, keys, values, offsets, out_weight):
    n = [2 * k for k in KEPT]
    bf = [
        (ROWS, WIDTH), (ROWS, WIDTH), (ROWS, WIDTH), (3, ROWS, HALF), (2, 3, ROWS, HALF), (2, n[1], HALF),
        (2, 2, 3, 2, KEPT[2], 128), (4, 2, 2, KEPT[3], HALF), (4, 2, 2, KEPT[4], HALF),
        (3, 2, KEPT[2], 128), (2, KEPT[3], HALF), (2, KEPT[4], HALF),
        (n[1], HALF), (n[2], HALF), (2 * n[3], HALF), (4, n[4], HALF),
    ]
    scratch = [pltpu.VMEM((5, 16), jnp.int32)] + [pltpu.VMEM(shape, BF) for shape in bf]
    for width in (HALF, 128, 128):
        scratch += [pltpu.VMEM(shape, F32) for shape in [
            (2, ROWS, width), (n[1], width), (n[2], width), (2 * n[3], width), (4 * n[4], width)]]
    scratch += [
        pltpu.VMEM((n[3], HALF), BF), pltpu.VMEM((n[3], 128), F32), pltpu.VMEM((n[3], 128), F32),
        pltpu.VMEM((n[3], HALF), BF), pltpu.VMEM((n[3], HALF), BF),
        pltpu.VMEM((32, 128), F32), pltpu.VMEM((32, 128), F32),
        pltpu.VMEM((3 * n[4], HALF), BF), pltpu.VMEM((2, 32, 128), F32), pltpu.VMEM((3, n[4], HALF), BF), pltpu.VMEM((3, 32, 128), F32),
        pltpu.VMEM((n[4], HALF), F32), pltpu.VMEM((n[4], 128), F32), pltpu.VMEM((n[4], 128), F32),
        pltpu.VMEM((ROWS, ROWS), BF),
        pltpu.VMEM((ROWS, HALF), BF),
        pltpu.SemaphoreType.DMA((4,)),
        pltpu.SemaphoreType.DMA((36,)),
        pltpu.SemaphoreType.DMA((36,)),
    ]
    vmem = pl.BlockSpec(memory_space=pltpu.VMEM)
    anywhere = pl.BlockSpec(memory_space=pl.ANY)
    merged = pl.pallas_call(
        kernel,
        out_shape=pltpu.VMEM((ROWS, WIDTH), BF),
        in_specs=[anywhere] * 4,
        out_specs=vmem,
        scratch_shapes=scratch,
        compiler_params=pltpu.CompilerParams(collective_id=0, has_side_effects=True, vmem_limit_bytes=40 << 20),
        cost_estimate=pl.CostEstimate(flops=3 * 10**9, bytes_accessed=5 * 10**6, transcendentals=9 * 10**6),
        name="dilated_attention",
    )(*[pltpu.with_memory_space_constraint(x, pltpu.HBM) for x in (offsets, queries, keys, values)])
    return pl.pallas_call(
        project,
        out_shape=jax.ShapeDtypeStruct((ROWS, WIDTH), BF),
        in_specs=[vmem, vmem],
        out_specs=anywhere,
        scratch_shapes=[pltpu.VMEM((ROWS, WIDTH), BF), pltpu.SemaphoreType.DMA((2,))],
        compiler_params=pltpu.CompilerParams(vmem_limit_bytes=16 << 20),
        name="projection",
    )(merged, pltpu.with_memory_space_constraint(out_weight, pltpu.VMEM))


def solution(mesh):
    return jax.shard_map(
        body,
        mesh=mesh,
        in_specs=(P(("dp", "seq"), None), P(("dp", "seq"), None), P(("dp", "seq"), None), P(), P()),
        out_specs=P(("dp", "seq"), None),
        check_vma=False,
    )
```
